32 devices in a mesh: seq: 8 (over y, x, core), section: 4 (over z).
Axes of the slice: x: 2, y: 2, z: 4, core: 2. Of those that a mesh axis runs over, the one named last changes fastest.
Arguments:
- cotangent: bfloat16 [1, 1024, 768], P(None, 'seq'), may hold values from -6 to 6
- projected: bfloat16 [4, 1, 1024, 2304], P('section', None, 'seq'), may hold values from -6 to 6
- w_in: bfloat16 [4, 768, 2304], P('section'), may hold values from -0.21875 to 0.21875
- w_out: bfloat16 [4, 768, 768], P('section'), may hold values from -0.078125 to 0.078125
- short_filter: float32 [4, 3, 2304], P('section'), may hold values from -3.5 to 3.5
- long_filter: float32 [4, 1024, 768], P('section', 'seq'), may hold values from -1.1 to 1.1, as said below
- filter_bias: float32 [4, 768], P('section'), may hold values from 0.3 to 0.9
Outputs:
- grads: bfloat16 [4, 1, 1024, 768], P('section', None, 'seq')
The draws below stay inside these ranges and needn't reach their ends.
Inputs may be any that keep to these rules, and one draw needn't show every extreme that they name: `long_filter`: row t of a section's long filter is its response at lag t.
All inputs are finite; a program needn't handle non-finite values.
Results may differ from the reference program's by a relative error of at most 0.03.
Values may be sent and summed in bfloat16 or wider, within the bound.
No kernel may reach another device: no remote copies, remote signals or barrier semaphores. Data moves between devices by JAX's collectives and lax.ppermute only.
A program may use at most 64 MiB of HBM per device.

```python
import math
import jax
import jax.numpy as jnp

D = 768
TAPS = 3
MICRO = 1
SECTIONS = 4
SEQ = 1024


def draw_long_filter(key, part):
    keys = jax.random.split(key, 7)
    lags = jnp.arange(SEQ, dtype=jnp.float32)[None, :, None]
    noise = jnp.clip(jax.random.normal(keys[0], (SECTIONS, SEQ, D), jnp.float32), -3.8, 3.8)
    slow_share = 0.5
    slow = jax.random.uniform(keys[1], (SECTIONS, 1, D), jnp.float32) < slow_share
    slow_rate = jnp.exp(jax.random.uniform(keys[2], (SECTIONS, 1, D), jnp.float32, math.log(0.2), 0.0)) / SEQ
    fast_rate = jnp.exp(jax.random.uniform(keys[3], (SECTIONS, 1, D), jnp.float32, math.log(1.0 / 50.0), math.log(1.0 / 30.0)))
    head_rate = jnp.where(slow, slow_rate, fast_rate)
    tail_rate = jnp.exp(jax.random.uniform(keys[5], (SECTIONS, 1, D), jnp.float32, math.log(0.1), math.log(0.5))) / SEQ
    tail_share = jnp.exp(jax.random.uniform(keys[6], (SECTIONS, 1, D), jnp.float32, 0.0, math.log(2.0)))
    head_power = 2.0 * head_rate * jnp.exp(-2.0 * head_rate * lags)
    tail_norm = 2.0 * tail_rate * tail_share / (1.0 - jnp.exp(-2.0 * tail_rate * SEQ))
    tail_power = tail_norm * jnp.exp(-2.0 * tail_rate * lags)
    marks = jax.random.randint(keys[4], (SECTIONS, 1, 1, 3), 1, SEQ).astype(jnp.float32)
    count = jnp.sum((lags[..., None] >= marks).astype(jnp.float32), axis=-1)
    envelope = jnp.sqrt(head_power + tail_power) * jnp.power(0.7, count)
    return noise * envelope


def steps_of(own_key, extent, cuts, low, top_value):
    factor_of = 1.0
    for axis_at, blocks in cuts:
        heights = jax.random.uniform(jax.random.fold_in(jax.random.fold_in(own_key, 6), axis_at), (blocks,), jnp.float32, low / len(cuts), top_value / len(cuts))
        factor_of = factor_of * jnp.repeat(jnp.exp(heights), extent[axis_at] // blocks).reshape((-1,) + (1,) * (len(extent) - 1 - axis_at))
    return factor_of


def bell_draw(own_key, extent, scale, limit, cuts=(), kind=jnp.bfloat16):
    loudness = steps_of(own_key, extent, cuts, -0.22, 0.18) if cuts else 1.0
    result = jax.random.normal(own_key, extent, jnp.float32) * scale * loudness
    return jnp.minimum(jnp.maximum(result, -limit), limit).astype(kind)


def setup_inputs(seed: int = 0) -> dict:
    splits = jax.random.split(jax.random.key(seed), 8)
    return {
        "cotangent": bell_draw(splits[0], (MICRO, SEQ, D), 1.0, 6.0, ((1, 8),)),
        "projected": bell_draw(splits[1], (SECTIONS, MICRO, SEQ, 3 * D), 1.0, 6.0, ((0, 4), (2, 8))),
        "w_in": bell_draw(splits[2], (SECTIONS, D, 3 * D), D ** -0.5, 0.21875, ((0, 4),)),
        "w_out": bell_draw(splits[3], (SECTIONS, D, D), (2 * SECTIONS * D) ** -0.5, 0.078125, ((0, 4),)),
        "short_filter": bell_draw(splits[4], (SECTIONS, TAPS, 3 * D), TAPS ** -0.5, 3.5, ((0, 4),), jnp.float32),
        "long_filter": draw_long_filter(jax.random.fold_in(splits[7], 71), 0),
        "filter_bias": jnp.clip(0.3 + 0.59999996 * jax.random.uniform(splits[6], (SECTIONS, D), jnp.float32) ** steps_of(splits[6], (SECTIONS, D), ((0, 4),), -0.2, 0.2), 0.3, 0.9),
    }


def causal_conv(response, series):
    size = 2 * series.shape[0]
    spectrum = jnp.fft.rfft(response, n=size, axis=0) * jnp.fft.rfft(series, n=size, axis=0)
    return jnp.fft.irfft(spectrum, n=size, axis=0)[:series.shape[0]]

def causal_corr(response, series):
    size = 2 * series.shape[0]
    spectrum = jnp.conj(jnp.fft.rfft(response, n=size, axis=0)) * jnp.fft.rfft(series, n=size, axis=0)
    return jnp.fft.irfft(spectrum, n=size, axis=0)[:series.shape[0]]

def section_grad(incoming, stored, weight_in, weight_out, taps, response, bias):
    width = weight_out.shape[0]
    zero_rows = jnp.zeros((2, stored.shape[1]), jnp.float32)
    padded = jnp.concatenate([zero_rows, stored.astype(jnp.float32)], axis=0)
    mixed = taps[0] * padded[2:] + taps[1] * padded[1:-1] + taps[2] * padded[:-2]
    query = mixed[:, :width]
    keys = mixed[:, width:2 * width]
    values = mixed[:, 2 * width:]
    product = (keys * values).astype(jnp.bfloat16)
    product_wide = product.astype(jnp.float32)
    conv = (causal_conv(response, product_wide) + bias * product_wide).astype(jnp.bfloat16)
    d_out = jnp.dot(incoming, weight_out.T, preferred_element_type=jnp.float32)
    d_conv = (d_out * query).astype(jnp.bfloat16)
    d_conv_wide = d_conv.astype(jnp.float32)
    d_prod = (causal_corr(response, d_conv_wide) + bias * d_conv_wide).astype(jnp.bfloat16)
    d_prod_wide = d_prod.astype(jnp.float32)
    d_mixed = jnp.concatenate([d_out * conv.astype(jnp.float32), d_prod_wide * values, d_prod_wide * keys], axis=1).astype(jnp.bfloat16)
    padded_grad = jnp.concatenate([d_mixed.astype(jnp.float32), zero_rows], axis=0)
    d_proj = (taps[0] * padded_grad[:-2] + taps[1] * padded_grad[1:-1] + taps[2] * padded_grad[2:]).astype(jnp.bfloat16)
    total = incoming.astype(jnp.float32) + jnp.dot(d_proj, weight_in.T, preferred_element_type=jnp.float32)
    return total.astype(jnp.bfloat16)

def reference(cotangent, projected, w_in, w_out, short_filter, long_filter, filter_bias):
    results = [None] * SECTIONS
    incoming = [cotangent[batch] for batch in range(MICRO)]
    for section in range(SECTIONS - 1, -1, -1):
        outputs = [section_grad(incoming[batch], projected[section, batch], w_in[section], w_out[section], short_filter[section], long_filter[section], filter_bias[section]) for batch in range(MICRO)]
        results[section] = jnp.stack(outputs)
        incoming = outputs
    return jnp.stack(results)
```

```python
import math

import jax
import jax.numpy as jnp
import numpy as np
from jax import lax
from jax.experimental import pallas as pl
from jax.experimental.pallas import tpu as pltpu
from jax.sharding import PartitionSpec as P

f32 = jnp.float32
bf16 = jnp.bfloat16
PAD = 16
CONTRACT = (((1,), (1,)), ((), ()))


def tables(rows):
    period = 2 * rows + 2 * PAD
    half = period // 2
    freq = 2.0 * math.pi * (np.arange(half) + 0.5) / period

    def forward(index):
        angle = np.outer(freq, index)
        return np.concatenate([np.cos(angle), -np.sin(angle)], axis=0)

    series = forward(np.arange(rows + PAD))
    lags = forward(np.arange(period) - (rows + PAD))
    angle = np.outer(np.arange(rows + PAD), freq)
    inverse = np.concatenate([np.cos(angle), -np.sin(angle)], axis=1) * (2.0 / period)
    return tuple(jnp.asarray(t.astype(np.float32), dtype=bf16) for t in (series, lags, inverse))


def dot(a, b):
    return jnp.dot(a, b, preferred_element_type=f32)


def lanes(part, width, core):
    half = width // 2
    return pl.ds(pl.multiple_of(part * width + core * half, 128), half)


def call(body, outs, scratch, name, n_in, smem=1, anys=()):
    specs = []
    for i in range(n_in):
        if i < smem:
            specs.append(pl.BlockSpec(memory_space=pltpu.SMEM))
        elif i in anys:
            specs.append(pl.BlockSpec(memory_space=pl.ANY))
        else:
            specs.append(pl.BlockSpec(memory_space=pltpu.VMEM))
    return pl.pallas_call(
        body,
        out_shape=outs,
        in_specs=specs,
        out_specs=jax.tree.map(lambda _: pl.BlockSpec(memory_space=pltpu.VMEM), outs),
        scratch_shapes=scratch,
        compiler_params=pltpu.CompilerParams(vmem_limit_bytes=56 * 1024 * 1024),
        name=name,
    )


def mix_stored(place, proj_own, proj_core, rim_own, rim_core, taps, query, keys, values, product, padded):
    core = place[1]
    rows = query.shape[0]
    own = rows // 2
    width = 2 * query.shape[1]
    ext = rows + PAD
    for part in range(3):
        at = lanes(part, width, core)
        here = pl.ds(part * (width // 2), width // 2)
        before = jnp.where(core == 0, rim_own[:, at], rim_core[:, at])
        after = jnp.where(core == 0, rim_core[:, at], rim_own[:, at])
        padded[0:PAD] = before.astype(f32)
        padded[pl.ds(pl.multiple_of(PAD + core * own, 16), own)] = proj_own[:, at].astype(f32)
        padded[pl.ds(pl.multiple_of(PAD + (1 - core) * own, 16), own)] = proj_core[:, here].astype(f32)
        padded[PAD + rows : 2 * PAD + rows] = after.astype(f32)
        size = rows if part == 0 else ext
        mixed = (
            taps[0:1, at] * padded[PAD : PAD + size]
            + taps[1:2, at] * padded[PAD - 1 : PAD - 1 + size]
            + taps[2:3, at] * padded[PAD - 2 : PAD - 2 + size]
        )
        (query, keys, values)[part][...] = mixed
    product[...] = (keys[...] * values[...]).astype(bf16)


def lag_spectra(place, count, *refs):
    pieces, (table, out, padded) = refs[:count], refs[count:]
    rows, chans = pieces[0].shape
    chip = place[0]
    ext = rows + PAD
    padded[0:ext] = jnp.zeros((ext, chans), bf16)
    padded[ext + count * rows :] = jnp.zeros((PAD, chans), bf16)
    for m in range(count):
        at = pl.multiple_of(ext + (chip ^ m) * rows, 16)
        padded[pl.ds(at, rows)] = pieces[m][...]
    for d in range(count):
        out[d] = dot(table[...], padded[pl.ds(d * rows, 2 * ext)])
    out[count] = jnp.zeros(out.shape[1:], f32)


def gate_grad(place, g_own, g_core, w_out, query, send, d_out):
    core = place[1]
    rows, chans = query.shape
    own = rows // 2
    weight = w_out[pl.ds(pl.multiple_of(core * chans, 16), chans)]
    for g, side in ((g_own, core), (g_core, 1 - core)):
        at = pl.ds(pl.multiple_of(side * own, 16), own)
        wide = lax.dot_general(g[...], weight, CONTRACT, preferred_element_type=f32)
        d_out[at] = wide
        send[at] = (wide * query[at]).astype(bf16)
    send[rows : rows + PAD] = d_out[0:PAD].astype(bf16)


def spectra_of(series, out, table):
    out[...] = dot(table[...], series)


def convolve(lag_ref, slots, spectra, adjoint, total, half):
    step = 16

    def tile(i, carry):
        upper = pl.ds(pl.multiple_of(i * step, step), step)
        lower = pl.ds(pl.multiple_of(half + i * step, step), step)
        real = imag = None
        for slot, at in zip(slots, spectra):
            lag_re, lag_im = lag_ref[slot, upper], lag_ref[slot, lower]
            ser_re, ser_im = at[upper], at[lower]
            if adjoint:
                re = lag_re * ser_re + lag_im * ser_im
                im = lag_re * ser_im - lag_im * ser_re
            else:
                re = lag_re * ser_re - lag_im * ser_im
                im = lag_re * ser_im + lag_im * ser_re
            real = re if real is None else real + re
            imag = im if imag is None else imag + im
        total[upper] = real.astype(bf16)
        total[lower] = imag.astype(bf16)
        return carry

    lax.fori_loop(0, half // step, tile, 0)


def input_grad(first, count, *refs):
    refs = list(refs)
    place, own, d_out = refs[:3]
    got = refs[3 : 2 + count]
    refs = refs[2 + count :]
    product = refs.pop(0) if first else None
    conv = None if first else refs.pop(0)
    lag_ref, series_table, inverse_table, keys, values, taps, bias, w_in, keep, pass_on = refs[:10]
    refs = refs[10:]
    if first:
        conv = refs.pop(0)
    weight, spec, total, mixed, d_proj, sums, sem = refs
    chip, core = place[0], place[1]
    rows, chans = d_out.shape
    own_rows = rows // 2
    width = 2 * chans
    ext = rows + PAD
    half = ext
    copies = [
        pltpu.make_async_copy(
            w_in.at[:, lanes(part, width, core)], weight.at[:, pl.ds(part * chans, chans)], sem.at[part]
        )
        for part in range(3)
    ]
    for copy in copies:
        copy.start()
    slot_of = lambda distance, valid: jnp.where(valid, distance, count)
    row_ids = lax.broadcasted_iota(jnp.int32, (ext, chans), 0)
    bias_here = bias[0:1, pl.ds(pl.multiple_of(core * chans, 128), chans)]
    for m in range(1, count):
        spec[m] = dot(series_table[:, 0:rows], got[m - 1][0:rows])
    spec[0] = dot(series_table[:, 0:rows], own[0:rows])
    if first:
        spec[count] = dot(series_table[...], product[...])
        slots = [jnp.int32(0)] + [slot_of(chip - (chip ^ m), (chip ^ m) < chip) for m in range(1, count)]
        convolve(lag_ref, slots, [spec.at[count]] + [spec.at[m] for m in range(1, count)], False, total, half)
        whole = dot(inverse_table[...], total[...]) + bias_here * product[...].astype(f32)
        conv[...] = whole.astype(bf16)
    slots = [jnp.int32(0)] + [slot_of((chip ^ m) - chip, (chip ^ m) > chip) for m in range(1, count)]
    convolve(lag_ref, slots, [spec.at[m] for m in range(count)], True, total, half)
    rim_conv = jnp.zeros((PAD, chans), f32)
    rim_out = jnp.zeros((PAD, chans), f32)
    for m in range(1, count):
        pick = ((chip ^ m) == chip + 1).astype(f32)
        rim_conv = rim_conv + pick * got[m - 1][0:PAD].astype(f32)
        rim_out = rim_out + pick * got[m - 1][rows : rows + PAD].astype(f32)
    inside = (chip < count - 1).astype(f32)
    mixed[0:rows] = bias_here * own[0:rows].astype(f32)
    mixed[rows:ext] = bias_here * rim_conv
    d_prod = (dot(inverse_table[...], total[...]) + mixed[...]).astype(bf16).astype(f32)
    d_prod = jnp.where(row_ids < rows, d_prod, d_prod * inside)
    for part in range(3):
        at = lanes(part, width, core)
        if part == 0:
            mixed[0:rows] = (d_out[...] * conv[0:rows].astype(f32)).astype(bf16).astype(f32)
            mixed[rows:ext] = (rim_out * conv[rows:ext].astype(f32)).astype(bf16).astype(f32)
        else:
            mixed[...] = (d_prod * (values if part == 1 else keys)[...]).astype(bf16).astype(f32)
        d_proj[:, pl.ds(part * chans, chans)] = (
            taps[0:1, at] * mixed[0:rows] + taps[1:2, at] * mixed[1 : rows + 1] + taps[2:3, at] * mixed[2 : rows + 2]
        ).astype(bf16)
    for copy in copies:
        copy.wait()
    sums[...] = lax.dot_general(d_proj[...], weight[...], CONTRACT, preferred_element_type=f32)
    keep[...] = sums[pl.ds(pl.multiple_of(core * own_rows, 16), own_rows)]
    pass_on[...] = sums[pl.ds(pl.multiple_of((1 - core) * own_rows, 16), own_rows)].astype(bf16)


def shards(cotangent, projected, w_in, w_out, short_filter, long_filter, filter_bias):
    seq_count = lax.axis_size("seq")
    section_count = lax.axis_size("section")
    seq_place = lax.axis_index("seq")
    section_place = lax.axis_index("section")
    chips = seq_count // 2
    chip, core = seq_place // 2, seq_place % 2
    place = jnp.stack([chip, core]).astype(jnp.int32)
    own_rows = projected.shape[2]
    rows = 2 * own_rows
    width = w_out.shape[2]
    chans = width // 2
    ext = rows + PAD
    half = ext
    series_table, lag_table, inverse_table = tables(rows)
    weight_in, weight_out, taps, bias = w_in[0], w_out[0], short_filter[0], filter_bias

    def swap_core(value):
        return lax.ppermute(value, "seq", [(i, i ^ 1) for i in range(seq_count)])

    def swap_chip(value, m):
        return lax.ppermute(value, "seq", [(i, ((i // 2) ^ m) * 2 + i % 2) for i in range(seq_count)])

    def half_of(value, part, side):
        return lax.dynamic_slice_in_dim(value, part * width + side * chans, chans, 1)

    def to_rows(own, other):
        return jnp.where(core == 0, jnp.concatenate([own, other]), jnp.concatenate([other, own]))

    lags = long_filter[0].astype(bf16)
    lags_core = swap_core(half_of(lags, 0, 1 - core))
    stored = projected[0, 0]
    rim_pairs = [(2 * q + 1, 2 * q + 2) for q in range(chips - 1)]
    rim_pairs += [(b, a) for a, b in rim_pairs]
    rim_own = lax.ppermute(jnp.where(core == 0, stored[:PAD], stored[own_rows - PAD :]), "seq", rim_pairs)
    stored_core = swap_core(jnp.concatenate([half_of(stored, part, 1 - core) for part in range(3)], axis=1))
    lags_here = to_rows(half_of(lags, 0, core), lags_core)
    pieces = [lags_here] + [swap_chip(lags_here, m) for m in range(1, chips)]
    rim_core = swap_core(rim_own)

    wide = lambda n, kind: jax.ShapeDtypeStruct((n, chans), kind)
    query, keys, values, product = call(
        mix_stored,
        [wide(rows, f32), wide(ext, f32), wide(ext, f32), wide(ext, bf16)],
        [pltpu.VMEM((rows + 2 * PAD, chans), f32)],
        "mix_stored",
        6,
    )(place, stored, stored_core, rim_own, rim_core, taps)

    spectra = call(
        lambda place, *refs: lag_spectra(place, chips, *refs),
        jax.ShapeDtypeStruct((chips + 1, 2 * half, chans), f32),
        [pltpu.VMEM((chips * rows + ext + PAD, chans), bf16)],
        "lag_spectra",
        2 + chips,
    )(place, *pieces, lag_table)

    grad = cotangent[0]
    result = jnp.zeros((own_rows, width), bf16)
    conv = None
    for turn in range(section_count):
        grad_core = swap_core(grad)
        block, d_out = call(
            gate_grad, [wide(ext, bf16), wide(rows, f32)], [], "gate_grad", 5
        )(place, grad, grad_core, weight_out, query)
        first = turn == 0
        got = []
        for m in range(1, chips):
            send = jnp.where((chip ^ m) > chip, product, block) if first else block
            got.append(swap_chip(send, m))
        outs = [jax.ShapeDtypeStruct((own_rows, width), f32), jax.ShapeDtypeStruct((own_rows, width), bf16)]
        if first:
            outs.append(wide(ext, bf16))
        n_in = 3 + (chips - 1) + 1 + 8
        answer = call(
            lambda *refs, first=first: input_grad(first, chips, *refs),
            outs,
            [
                pltpu.VMEM((width, 3 * chans), bf16),
                pltpu.VMEM((chips + 1, 2 * half, chans), f32),
                pltpu.VMEM((2 * half, chans), bf16),
                pltpu.VMEM((ext, chans), f32),
                pltpu.VMEM((rows, 3 * chans), bf16),
                pltpu.VMEM((rows, width), f32),
                pltpu.SemaphoreType.DMA((3,)),
            ],
            "input_grad_first" if first else "input_grad",
            n_in,
            anys=(n_in - 1,),
        )(
            place, block, d_out, *got, product if first else conv, spectra, series_table, inverse_table,
            keys, values, taps, bias, weight_in,
        )
        keep, pass_on = answer[:2]
        if first:
            conv = answer[2]
        total = (grad.astype(f32) + keep + swap_core(pass_on).astype(f32)).astype(bf16)
        upper = section_count - 1 - turn
        result = jnp.where(section_place == upper, total, result)
        if turn < section_count - 1:
            grad = lax.ppermute(total, "section", [(upper, upper - 1), (upper - 1, upper)])
    return result[None, None]


def solution(mesh):
    return jax.shard_map(
        shards,
        mesh=mesh,
        in_specs=(
            P(None, "seq", None),
            P("section", None, "seq", None),
            P("section", None, None),
            P("section", None, None),
            P("section", None, None),
            P("section", "seq", None),
            P("section", None),
        ),
        out_specs=P("section", None, "seq", None),
        check_vma=False,
    )
```

```python
import math

import jax
import jax.numpy as jnp
import numpy as np
from jax import lax
from jax.experimental import pallas as pl
from jax.experimental.pallas import tpu as pltpu
from jax.sharding import PartitionSpec as P

f32 = jnp.float32
bf16 = jnp.bfloat16
PAD = 16
CONTRACT = (((1,), (1,)), ((), ()))


def tables(rows):
    period = 2 * rows + 2 * PAD
    half = period // 2
    freq = 2.0 * math.pi * (np.arange(half) + 0.5) / period

    def forward(index):
        angle = np.outer(freq, index)
        return np.concatenate([np.cos(angle), -np.sin(angle)], axis=0)

    series = forward(np.arange(rows + PAD))
    lags = forward(np.arange(period) - (rows + PAD))
    angle = np.outer(np.arange(rows + PAD), freq)
    inverse = np.concatenate([np.cos(angle), -np.sin(angle)], axis=1) * (2.0 / period)
    return tuple(jnp.asarray(t.astype(np.float32), dtype=bf16) for t in (series, lags, inverse))


def dot(a, b):
    return jnp.dot(a, b, preferred_element_type=f32)


def dot_last(a, b):
    return lax.dot_general(a, b, CONTRACT, preferred_element_type=f32)


def lanes(part, width, core):
    half = width // 2
    return pl.ds(pl.multiple_of(part * width + core * half, 128), half)


def side_rows(side, own):
    return pl.ds(pl.multiple_of(side * own, 16), own)


def call(body, outs, scratch, name, limit, micros, place, *operands):
    vmem = pl.BlockSpec(memory_space=pltpu.VMEM)
    return pl.pallas_call(
        body,
        out_shape=outs,
        in_specs=[pl.BlockSpec(memory_space=pltpu.SMEM)] + [vmem] * len(operands),
        out_specs=jax.tree.map(lambda _: vmem, outs),
        scratch_shapes=scratch,
        compiler_params=pltpu.CompilerParams(vmem_limit_bytes=limit),
        cost_estimate=pl.CostEstimate(flops=int(micros * 1e9), bytes_accessed=0, transcendentals=0),
        name=name,
    )(place, *operands)


def split_lags(place, lags, own, other):
    core = place[1]
    own[...] = lags[:, lanes(0, lags.shape[1], core)].astype(bf16)
    other[...] = lags[:, lanes(0, lags.shape[1], 1 - core)].astype(bf16)


def split_stored(place, stored, grad, _, other, rim):
    core = place[1]
    rows, chans = other.shape[0], other.shape[1] // 3
    width = 2 * chans
    for part in range(3):
        other[:, part * chans : (part + 1) * chans] = stored[:, lanes(part, width, 1 - core)]
    edge = pl.ds(pl.multiple_of(core * (rows - PAD), 16), PAD)
    rim[:, : 3 * width] = stored[edge]
    rim[:, 3 * width :] = grad[edge]


def mix_stored(place, stored, stored_core, rim_own, rim_core, grad, taps, _, __, query, keys, values, product, grad_ext, padded):
    core = place[1]
    own, width = grad.shape
    rows = 2 * own
    ext = rows + PAD
    for part in range(3):
        at = lanes(part, width, core)
        here = pl.ds(part * (width // 2), width // 2)
        before = jnp.where(core == 0, rim_own[:, at], rim_core[:, at])
        before = jnp.where(place[0] == 0, jnp.zeros_like(before), before)
        after = jnp.where(core == 0, rim_core[:, at], rim_own[:, at])
        padded[0:PAD] = before.astype(f32)
        padded[pl.ds(pl.multiple_of(PAD + core * own, 16), own)] = stored[:, at].astype(f32)
        padded[pl.ds(pl.multiple_of(PAD + (1 - core) * own, 16), own)] = stored_core[:, here].astype(f32)
        padded[PAD + rows : 2 * PAD + rows] = after.astype(f32)
        mixed = (
            taps[0, :, at] * padded[PAD : PAD + ext]
            + taps[1, :, at] * padded[PAD - 1 : PAD - 1 + ext]
            + taps[2, :, at] * padded[PAD - 2 : PAD - 2 + ext]
        )
        (query, keys, values)[part][...] = mixed
    product[...] = (keys[...] * values[...]).astype(bf16)
    grad_ext[0:own] = grad[...]
    grad_ext[own:] = jnp.where(core == 0, rim_core[:, 3 * width :], rim_own[:, 3 * width :])


def lag_spectra(place, count, *refs):
    pieces, (table, out, padded) = refs[:count], refs[count:]
    rows, chans = pieces[0].shape
    chip = place[0]
    ext = rows + PAD
    padded[0:ext] = jnp.zeros((ext, chans), bf16)
    padded[ext + count * rows :] = jnp.zeros((PAD, chans), bf16)
    for m in range(count):
        at = pl.multiple_of(ext + (chip ^ m) * rows, 16)
        padded[pl.ds(at, rows)] = pieces[m][...]
    for d in range(count):
        out[d] = dot(table[...], padded[pl.ds(d * rows, 2 * ext)])
    out[count] = jnp.zeros(out.shape[1:], f32)


def gate_grad(place, g_own, g_core, w_out, query, block, upper, lower, rim, d_out):
    core = place[1]
    rows, chans = block.shape
    own = rows // 2
    weight = w_out[pl.ds(pl.multiple_of(core * chans, 16), chans)]
    wide = dot_last(g_own[...], weight)
    d_out[side_rows(core, own)] = wide[:own]
    d_out[rows:] = wide[own:]
    d_out[side_rows(1 - core, own)] = dot_last(g_core[0:own], weight)
    upper[...] = (d_out[0:own] * query[0:own]).astype(bf16)
    lower[...] = (d_out[own:rows] * query[own:rows]).astype(bf16)
    block[0:own] = upper[...]
    block[own:rows] = lower[...]
    rim[...] = (d_out[rows:] * query[rows:]).astype(bf16)


def slot_of(place, m, count, adjoint):
    chip, other = place[0], place[0] ^ m
    distance = other - chip if adjoint else chip - other
    return jnp.where(distance >= 0, distance, count)


def accumulate(lag_ref, pairs, adjoint, start, total):
    step = 16
    half = total.shape[0] // 2

    def tile(i, carry):
        upper = pl.ds(pl.multiple_of(i * step, step), step)
        lower = pl.ds(pl.multiple_of(half + i * step, step), step)
        real, imag = (None, None) if start is None else (start[upper], start[lower])
        for slot, at in pairs:
            lag_re, lag_im = lag_ref[slot, upper], lag_ref[slot, lower]
            ser_re, ser_im = at[upper], at[lower]
            if adjoint:
                re = lag_re * ser_re + lag_im * ser_im
                im = lag_re * ser_im - lag_im * ser_re
            else:
                re = lag_re * ser_re - lag_im * ser_im
                im = lag_re * ser_im + lag_im * ser_re
            real = re if real is None else real + re
            imag = im if imag is None else imag + im
        total[upper] = real.astype(total.dtype)
        total[lower] = imag.astype(total.dtype)
        return carry

    lax.fori_loop(0, half // step, tile, 0)


def short_adjoint(taps, at, mixed, ext):
    mixed[ext:] = jnp.zeros((PAD, mixed.shape[1]), f32)
    return (
        taps[0, :, at] * mixed[0:ext] + taps[1, :, at] * mixed[1 : ext + 1] + taps[2, :, at] * mixed[2 : ext + 2]
    ).astype(bf16)


def inside_rows(place, count, rows, ext, chans):
    ids = lax.broadcasted_iota(jnp.int32, (ext, chans), 0)
    return jnp.where((ids < rows) | (place[0] < count - 1), 1.0, 0.0)


def query_part(place, count, d_out, conv, taps, w_in, mixed, share):
    ext, chans = d_out.shape
    rows, width = ext - PAD, 2 * chans
    inside = inside_rows(place, count, rows, ext, chans)
    at = lanes(0, width, place[1])
    mixed[0:ext] = (d_out[...] * conv[...].astype(f32) * inside).astype(bf16).astype(f32)
    share[...] = dot_last(short_adjoint(taps, at, mixed, ext), w_in[:, at])


def gated_part(place, count, total, inverse, block, rim, keys, values, bias, taps, w_in, share, mixed, keep, pass_on):
    core = place[1]
    rows, chans = block.shape
    own, ext, width = rows // 2, rows + PAD, 2 * chans
    inside = inside_rows(place, count, rows, ext, chans)
    bias_here = bias[0:1, lanes(0, width, core)]
    mixed[0:rows] = bias_here * block[...].astype(f32)
    mixed[rows:ext] = bias_here * rim[...].astype(f32)
    d_prod = (dot(inverse[...], total[...]) + mixed[0:ext]).astype(bf16).astype(f32) * inside
    sums = share[...]
    for part, other in ((1, values), (2, keys)):
        at = lanes(part, width, core)
        mixed[0:ext] = (d_prod * other[...]).astype(bf16).astype(f32)
        sums = sums + dot_last(short_adjoint(taps, at, mixed, ext), w_in[:, at])
    share[...] = sums
    keep[0:own] = share[side_rows(core, own)]
    keep[own:] = share[rows:]
    pass_on[0:own] = share[side_rows(1 - core, own)].astype(bf16)
    pass_on[own:] = share[rows:].astype(bf16)


def early(place, count, block, d_out, conv, lag_ref, table, taps, w_in, total, share, spec, mixed):
    rows = block.shape[0]
    spec[...] = dot(table[:, 0:rows], block[...])
    accumulate(lag_ref, [(slot_of(place, 0, count, True), spec)], True, None, total)
    query_part(place, count, d_out, conv, taps, w_in, mixed, share)


def middle(place, count, ms, *refs):
    got, (start, lag_ref, table, total, spec) = refs[: len(ms)], refs[len(ms) :]
    pairs = []
    for i, m in enumerate(ms):
        spec[i] = dot(table[:, 0 : got[i].shape[0]], got[i][...])
        pairs.append((slot_of(place, m, count, True), spec.at[i]))
    accumulate(lag_ref, pairs, True, start, total)


def late_pairs(place, count, got, spec, table):
    rows = got[0].shape[0] if len(got) > 2 else 2 * got[0].shape[0]
    first = count - (len(got) - 1)
    pairs = []
    for i in range(len(got) - 1):
        if i < len(got) - 2:
            spec[i] = dot(table[:, 0:rows], got[i][...])
        else:
            half = rows // 2
            spec[i] = dot(table[:, 0:half], got[i][...]) + dot(table[:, half:rows], got[i + 1][...])
        pairs.append((first + i, spec.at[i]))
    return [[(slot_of(place, m, count, adjoint), at) for m, at in pairs] for adjoint in (False, True)]


def late(place, count, n_got, *refs):
    got, refs = refs[:n_got], refs[n_got:]
    start, part_share, block, rim, lag_ref, table, inverse, keys, values, bias, taps, w_in = refs[:12]
    keep, pass_on, spec, total, mixed, share = refs[12:]
    _, pairs = late_pairs(place, count, got, spec, table)
    accumulate(lag_ref, pairs, True, start, total)
    share[...] = part_share[...]
    gated_part(
        place, count, total, inverse, block, rim, keys, values, bias, taps, w_in, share, mixed, keep, pass_on
    )


def early_first(place, count, block, product, lag_ref, table, total, total_conv, spec):
    rows = block.shape[0]
    spec[...] = dot(table[:, 0:rows], block[...])
    accumulate(lag_ref, [(slot_of(place, 0, count, True), spec)], True, None, total)
    spec[...] = dot(table[...], product[...])
    accumulate(lag_ref, [(slot_of(place, 0, count, False), spec)], False, None, total_conv)


def middle_first(place, count, ms, *refs):
    got, (start, start_conv, lag_ref, table, total, total_conv, spec) = refs[: len(ms)], refs[len(ms) :]
    for i, m in enumerate(ms):
        spec[i] = dot(table[:, 0 : got[i].shape[0]], got[i][...])
    for adjoint, begin, end in ((True, start, total), (False, start_conv, total_conv)):
        pairs = [(slot_of(place, m, count, adjoint), spec.at[i]) for i, m in enumerate(ms)]
        accumulate(lag_ref, pairs, adjoint, begin, end)


def late_first(place, count, n_got, *refs):
    got, refs = refs[:n_got], refs[n_got:]
    start, start_conv, d_out, product, block, rim, lag_ref, table, inverse, keys, values, bias, taps, w_in = refs[:14]
    keep, pass_on, conv, spec, total, mixed, share = refs[14:]
    width = 2 * block.shape[1]
    pairs_conv, pairs = late_pairs(place, count, got, spec, table)
    accumulate(lag_ref, pairs_conv, False, start_conv, total)
    whole = dot(inverse[...], total[...]) + bias[0:1, lanes(0, width, place[1])] * product[...].astype(f32)
    conv[...] = whole.astype(bf16)
    query_part(place, count, d_out, conv, taps, w_in, mixed, share)
    accumulate(lag_ref, pairs, True, start, total)
    gated_part(
        place, count, total, inverse, block, rim, keys, values, bias, taps, w_in, share, mixed, keep, pass_on
    )


def shards(cotangent, projected, w_in, w_out, short_filter, long_filter, filter_bias):
    seq_count = lax.axis_size("seq")
    section_count = lax.axis_size("section")
    seq_place = lax.axis_index("seq")
    section_place = lax.axis_index("section")
    chips = seq_count // 2
    core = seq_place % 2
    place = jnp.stack([seq_place // 2, core]).astype(jnp.int32)
    own_rows = projected.shape[2]
    rows = 2 * own_rows
    width = w_out.shape[2]
    chans = width // 2
    ext = rows + PAD
    limit = (8 + 3 * chips) * 1024 * 1024
    table, lag_table, inverse = tables(rows)
    weight_in, weight_out, bias = w_in[0], w_out[0], filter_bias
    taps = jnp.transpose(short_filter, (1, 0, 2))

    def swap_core(value):
        return lax.ppermute(value, "seq", [(i, i ^ 1) for i in range(seq_count)])

    def swap_chip(value, m):
        return lax.ppermute(value, "seq", [(i, ((i // 2) ^ m) * 2 + i % 2) for i in range(seq_count)])

    def swap_section(value, upper):
        pairs = []
        for i in range(seq_count):
            for s in range(section_count):
                t = s - 1 if (s - upper) % 2 == 0 else s + 1
                j, t = (i, t) if 0 <= t < section_count else (i ^ 1, s)
                pairs.append((i * section_count + s, j * section_count + t))
        return lax.ppermute(value, ("seq", "section"), pairs)

    def shape(n, kind, across=chans):
        return jax.ShapeDtypeStruct((n, across), kind)

    def run(body, outs, scratch, name, micros, *operands):
        return call(body, outs, scratch, name, limit, micros, place, *operands)

    stored, grad = projected[0, 0], cotangent[0]
    lags_own, lags_other = run(
        split_lags, [shape(own_rows, bf16), shape(own_rows, bf16)], [], "split_lags", 0.4, long_filter[0]
    )
    stored_other, rim_send = run(
        split_stored, [shape(own_rows, bf16, 3 * chans), shape(PAD, bf16, 4 * width)], [], "split_stored", 0.6,
        stored, grad, lags_other,
    )
    lags_core = swap_core(lags_other)
    rim_pairs = [(2 * q + 1, (2 * q + 2) % seq_count) for q in range(chips)]
    rim_own = lax.ppermute(rim_send, "seq", rim_pairs + [(b, a) for a, b in rim_pairs])
    lags_here = jnp.where(
        core == 0, jnp.concatenate([lags_own, lags_core]), jnp.concatenate([lags_core, lags_own])
    )
    pieces = [lags_here] + [swap_chip(lags_here, m) for m in range(1, chips)]
    stored_core = swap_core(stored_other)
    grad_core = swap_core(grad)
    rim_core = swap_core(rim_own)
    query, keys, values, product, grad = run(
        mix_stored,
        [shape(ext, f32), shape(ext, f32), shape(ext, f32), shape(ext, bf16), shape(own_rows + PAD, bf16, width)],
        [pltpu.VMEM((rows + 2 * PAD, chans), f32)],
        "mix_stored", 1.3,
        stored, stored_core, rim_own, rim_core, grad, taps, pieces[1], pieces[2],
    )
    spectra = run(
        lambda place, *refs: lag_spectra(place, chips, *refs),
        jax.ShapeDtypeStruct((chips + 1, 2 * ext, chans), f32),
        [pltpu.VMEM((chips * rows + ext + PAD, chans), bf16)],
        "lag_spectra", 2.4,
        *pieces, lag_table,
    )

    spec = pltpu.VMEM((2 * ext, chans), f32)
    total_wide = shape(2 * ext, f32)
    total_scratch = pltpu.VMEM((2 * ext, chans), bf16)
    mixed = pltpu.VMEM((ext + PAD, chans), f32)
    share = pltpu.VMEM((ext, width), f32)
    ms = list(range(1, chips // 2))
    specs = pltpu.VMEM((len(ms), 2 * ext, chans), f32)
    late_specs = pltpu.VMEM((chips - 1 - len(ms), 2 * ext, chans), f32)
    ends = [shape(own_rows + PAD, f32, width), shape(own_rows + PAD, bf16, width)]
    result = jnp.zeros((own_rows, width), bf16)
    conv = None
    for turn in range(section_count):
        first = turn == 0
        block, upper_half, lower_half, rim, d_out = run(
            gate_grad,
            [shape(rows, bf16), shape(own_rows, bf16), shape(own_rows, bf16), shape(PAD, bf16), shape(ext, f32)],
            [],
            "gate_grad", 1.0,
            grad, grad_core if first else swap_core(grad), weight_out, query,
        )

        def send(value, at, m):
            if first:
                value = jnp.where(((seq_place // 2) ^ m) > seq_place // 2, product[at], value)
            return swap_chip(value, m)

        got = [send(block, slice(0, rows), m) for m in range(1, chips - 1)]
        got.append(send(upper_half, slice(0, own_rows), chips - 1))
        got.append(send(lower_half, slice(own_rows, rows), chips - 1))
        soon, last = got[: len(ms)], got[len(ms) :]
        if first:
            start, start_conv = run(
                lambda place, *refs: early_first(place, chips, *refs),
                [total_wide, total_wide], [spec], "early_first", 1.8, block, product, spectra, table,
            )
            start, start_conv = run(
                lambda place, *refs: middle_first(place, chips, ms, *refs),
                [total_wide, total_wide], [specs], "middle_first", 1.0, *soon, start, start_conv, spectra, table,
            )
            keep, pass_on, conv = run(
                lambda place, *refs: late_first(place, chips, len(last), *refs),
                ends + [shape(ext, bf16)], [late_specs, total_scratch, mixed, share], "late_first", 4.0,
                *last, start, start_conv, d_out, product, block, rim, spectra, table, inverse, keys, values, bias,
                taps, weight_in,
            )
        else:
            start, part_share = run(
                lambda place, *refs: early(place, chips, *refs),
                [total_wide, shape(ext, f32, width)], [spec, mixed], "early", 1.6,
                block, d_out, conv, spectra, table, taps, weight_in,
            )
            start = run(
                lambda place, *refs: middle(place, chips, ms, *refs),
                total_wide, [specs], "middle", 0.8, *soon, start, spectra, table,
            )
            keep, pass_on = run(
                lambda place, *refs: late(place, chips, len(last), *refs),
                ends, [late_specs, total_scratch, mixed, share], "late", 3.0,
                *last, start, part_share, block, rim, spectra, table, inverse, keys, values, bias, taps, weight_in,
            )
        summed = (grad.astype(f32) + keep + swap_core(pass_on).astype(f32)).astype(bf16)
        upper = section_count - 1 - turn
        result = jnp.where(section_place == upper, summed[:own_rows], result)
        if turn < section_count - 1:
            grad = swap_section(summed, upper)
    return result[None, None]


def solution(mesh):
    return jax.shard_map(
        shards,
        mesh=mesh,
        in_specs=(
            P(None, "seq", None),
            P("section", None, "seq", None),
            P("section", None, None),
            P("section", None, None),
            P("section", None, None),
            P("section", "seq", None),
            P("section", None),
        ),
        out_specs=P("section", None, "seq", None),
        check_vma=False,
    )
```

```python
import math

import jax
import jax.numpy as jnp
import numpy as np
from jax import lax
from jax.experimental import pallas as pl
from jax.experimental.pallas import tpu as pltpu
from jax.sharding import PartitionSpec as P

f32 = jnp.float32
bf16 = jnp.bfloat16
PAD = 16
CONTRACT = (((1,), (1,)), ((), ()))


def tables(rows):
    period = 2 * rows + 2 * PAD
    half = period // 2
    freq = 2.0 * math.pi * (np.arange(half) + 0.5) / period

    def forward(index):
        angle = np.outer(freq, index)
        return np.concatenate([np.cos(angle), -np.sin(angle)], axis=0)

    series = forward(np.arange(rows + PAD))
    lags = forward(np.arange(period) - (rows + PAD))
    angle = np.outer(np.arange(rows + PAD), freq)
    inverse = np.concatenate([np.cos(angle), -np.sin(angle)], axis=1) * (2.0 / period)
    return tuple(jnp.asarray(t.astype(np.float32), dtype=bf16) for t in (series, lags, inverse))


def dot(a, b):
    return jnp.dot(a, b, preferred_element_type=f32)


def dot_last(a, b):
    return lax.dot_general(a, b, CONTRACT, preferred_element_type=f32)


def lanes(part, width, core):
    half = width // 2
    return pl.ds(pl.multiple_of(part * width + core * half, 128), half)


def side_rows(side, own):
    return pl.ds(pl.multiple_of(side * own, 16), own)


def call(body, outs, scratch, name, limit, micros, *operands):
    vmem = pl.BlockSpec(memory_space=pltpu.VMEM)

    def placed(*refs):
        seq = lax.axis_index("seq")
        body((seq // 2, seq % 2), *refs)

    return pl.pallas_call(
        placed,
        out_shape=outs,
        in_specs=[vmem] * len(operands),
        out_specs=jax.tree.map(lambda _: vmem, outs),
        scratch_shapes=scratch,
        compiler_params=pltpu.CompilerParams(vmem_limit_bytes=limit),
        cost_estimate=pl.CostEstimate(flops=int(micros * 1e9), bytes_accessed=0, transcendentals=0),
        name=name,
    )(*operands)


def split_lags(place, lags, own, other):
    core = place[1]
    own[...] = lags[:, lanes(0, lags.shape[1], core)].astype(bf16)
    other[...] = lags[:, lanes(0, lags.shape[1], 1 - core)].astype(bf16)


def split_stored(place, stored, grad, _, other, rim):
    core = place[1]
    rows, chans = other.shape[0], other.shape[1] // 3
    width = 2 * chans
    for part in range(3):
        other[:, part * chans : (part + 1) * chans] = stored[:, lanes(part, width, 1 - core)]
    edge = pl.ds(pl.multiple_of(core * (rows - PAD), 16), PAD)
    rim[:, : 3 * width] = stored[edge]
    rim[:, 3 * width :] = grad[edge]


def mix_stored(place, stored, stored_core, rim_own, rim_core, grad, taps, _, __, query, keys, values, product, grad_ext, padded):
    core = place[1]
    own, width = grad.shape
    rows = 2 * own
    ext = rows + PAD
    for part in range(3):
        at = lanes(part, width, core)
        here = pl.ds(part * (width // 2), width // 2)
        before = jnp.where(core == 0, rim_own[:, at], rim_core[:, at])
        before = jnp.where(place[0] == 0, jnp.zeros_like(before), before)
        after = jnp.where(core == 0, rim_core[:, at], rim_own[:, at])
        padded[0:PAD] = before.astype(f32)
        padded[pl.ds(pl.multiple_of(PAD + core * own, 16), own)] = stored[:, at].astype(f32)
        padded[pl.ds(pl.multiple_of(PAD + (1 - core) * own, 16), own)] = stored_core[:, here].astype(f32)
        padded[PAD + rows : 2 * PAD + rows] = after.astype(f32)
        mixed = (
            taps[0, :, at] * padded[PAD : PAD + ext]
            + taps[1, :, at] * padded[PAD - 1 : PAD - 1 + ext]
            + taps[2, :, at] * padded[PAD - 2 : PAD - 2 + ext]
        )
        (query, keys, values)[part][...] = mixed
    product[...] = (keys[...] * values[...]).astype(bf16)
    grad_ext[0:own] = grad[...]
    grad_ext[own:] = jnp.where(core == 0, rim_core[:, 3 * width :], rim_own[:, 3 * width :])


def lag_spectra(place, count, *refs):
    pieces, (table, out, padded) = refs[:count], refs[count:]
    rows, chans = pieces[0].shape
    chip = place[0]
    ext = rows + PAD
    padded[0:ext] = jnp.zeros((ext, chans), bf16)
    padded[ext + count * rows :] = jnp.zeros((PAD, chans), bf16)
    for m in range(count):
        at = pl.multiple_of(ext + (chip ^ m) * rows, 16)
        padded[pl.ds(at, rows)] = pieces[m][...]
    for d in range(count):
        out[d] = dot(table[...], padded[pl.ds(d * rows, 2 * ext)])
    out[count] = jnp.zeros(out.shape[1:], f32)


def gate_grad(place, g_own, g_core, w_out, query, block, upper, lower, rim, d_out):
    core = place[1]
    rows, chans = block.shape
    own = rows // 2
    weight = w_out[pl.ds(pl.multiple_of(core * chans, 16), chans)]
    wide = dot_last(g_own[...], weight)
    d_out[side_rows(core, own)] = wide[:own]
    d_out[rows:] = wide[own:]
    d_out[side_rows(1 - core, own)] = dot_last(g_core[0:own], weight)
    upper[...] = (d_out[0:own] * query[0:own]).astype(bf16)
    lower[...] = (d_out[own:rows] * query[own:rows]).astype(bf16)
    block[0:own] = upper[...]
    block[own:rows] = lower[...]
    rim[...] = (d_out[rows:] * query[rows:]).astype(bf16)


def gate_only(place, d_out, query, _, block, upper, lower, rim):
    rows = block.shape[0]
    own = rows // 2
    d_conv = (d_out[...].astype(f32) * query[...]).astype(bf16)
    upper[...] = d_conv[0:own]
    lower[...] = d_conv[own:rows]
    block[...] = d_conv[0:rows]
    rim[...] = d_conv[rows:]


def carry_grad(place, g_own, g_core, below, _, out):
    core = place[1]
    rows = out.shape[0] - PAD
    own = rows // 2
    wide = dot_last(g_own[...], below[...])
    out[side_rows(core, own)] = wide[:own]
    out[rows:] = wide[own:]
    out[side_rows(1 - core, own)] = dot_last(g_core[0:own], below[...])


def split_rows(place, share, _, keep, pass_on):
    rows = share.shape[0] - PAD
    own = rows // 2
    keep[0:own] = share[side_rows(place[1], own)]
    keep[own:] = share[rows:]
    pass_on[0:own] = share[side_rows(1 - place[1], own)].astype(bf16)
    pass_on[own:] = share[rows:].astype(bf16)


def keep_half(place, short_share, below, carried, keep):
    keep[...] = carried[...] + dot_last(short_share[...], below[...])


def pass_half(place, short_share, below_core, pass_on):
    pass_on[...] = dot_last(short_share[...], below_core[...]).astype(bf16)


def slot_of(place, m, count, adjoint):
    chip, other = place[0], place[0] ^ m
    distance = other - chip if adjoint else chip - other
    return jnp.where(distance >= 0, distance, count)


def accumulate(lag_ref, pairs, adjoint, start, total):
    step = 16
    half = total.shape[0] // 2

    def tile(i, carry):
        upper = pl.ds(pl.multiple_of(i * step, step), step)
        lower = pl.ds(pl.multiple_of(half + i * step, step), step)
        real, imag = (None, None) if start is None else (start[upper], start[lower])
        for slot, at in pairs:
            lag_re, lag_im = lag_ref[slot, upper], lag_ref[slot, lower]
            ser_re, ser_im = at[upper], at[lower]
            if adjoint:
                re = lag_re * ser_re + lag_im * ser_im
                im = lag_re * ser_im - lag_im * ser_re
            else:
                re = lag_re * ser_re - lag_im * ser_im
                im = lag_re * ser_im + lag_im * ser_re
            real = re if real is None else real + re
            imag = im if imag is None else imag + im
        total[upper] = real.astype(total.dtype)
        total[lower] = imag.astype(total.dtype)
        return carry

    lax.fori_loop(0, half // step, tile, 0)


def short_adjoint(taps, at, mixed, ext):
    mixed[ext:] = jnp.zeros((PAD, mixed.shape[1]), f32)
    return (
        taps[0, :, at] * mixed[0:ext] + taps[1, :, at] * mixed[1 : ext + 1] + taps[2, :, at] * mixed[2 : ext + 2]
    ).astype(bf16)


def inside_rows(place, count, rows, ext, chans):
    ids = lax.broadcasted_iota(jnp.int32, (ext, chans), 0)
    return jnp.where((ids < rows) | (place[0] < count - 1), 1.0, 0.0)


def query_part(place, count, d_out, conv, taps, mixed, proj_query):
    ext, chans = d_out.shape
    rows, width = ext - PAD, 2 * chans
    inside = inside_rows(place, count, rows, ext, chans)
    at = lanes(0, width, place[1])
    mixed[0:ext] = (d_out[...].astype(f32) * conv[...].astype(f32) * inside).astype(bf16).astype(f32)
    proj_query[...] = short_adjoint(taps, at, mixed, ext)


def gated_part(
    place, count, total, inverse, block, rim, keys, values, bias, taps, mixed, proj, w_in, part_share, share, short_share
):
    core = place[1]
    rows, chans = block.shape
    ext, width = rows + PAD, 2 * chans
    inside = inside_rows(place, count, rows, ext, chans)
    bias_here = bias[0:1, lanes(0, width, core)]
    mixed[0:rows] = bias_here * block[...].astype(f32)
    mixed[rows:ext] = bias_here * rim[...].astype(f32)
    d_prod = (dot(inverse[...], total[...]) + mixed[0:ext]).astype(bf16).astype(f32) * inside
    sums = part_share[...]
    for part, other in ((1, values), (2, keys)):
        at = lanes(part, width, core)
        mixed[0:ext] = (d_prod * other[...]).astype(bf16).astype(f32)
        proj[...] = short_adjoint(taps, at, mixed, ext)
        sums = sums + dot_last(proj[...], w_in[:, at])
    share[...] = sums
    short_share[...] = sums.astype(bf16)


def early(place, count, block, d_out, conv, lag_ref, table, taps, w_in, total, share, spec, mixed, proj):
    rows = block.shape[0]
    spec[...] = dot(table[:, 0:rows], block[...])
    accumulate(lag_ref, [(slot_of(place, 0, count, True), spec)], True, None, total)
    query_part(place, count, d_out, conv, taps, mixed, proj)
    share[...] = dot_last(proj[...], w_in[:, lanes(0, w_in.shape[0], place[1])])


def middle(place, count, ms, *refs):
    got, (start, lag_ref, table, total, spec) = refs[: len(ms)], refs[len(ms) :]
    pairs = []
    for i, m in enumerate(ms):
        spec[i] = dot(table[:, 0 : got[i].shape[0]], got[i][...])
        pairs.append((slot_of(place, m, count, True), spec.at[i]))
    accumulate(lag_ref, pairs, True, start, total)


def late_pairs(place, count, got, spec, table):
    rows = got[0].shape[0] if len(got) > 2 else 2 * got[0].shape[0]
    first = count - (len(got) - 1)
    pairs = []
    for i in range(len(got) - 1):
        if i < len(got) - 2:
            spec[i] = dot(table[:, 0:rows], got[i][...])
        else:
            half = rows // 2
            spec[i] = dot(table[:, 0:half], got[i][...]) + dot(table[:, half:rows], got[i + 1][...])
        pairs.append((first + i, spec.at[i]))
    return [[(slot_of(place, m, count, adjoint), at) for m, at in pairs] for adjoint in (False, True)]


def late(place, count, n_got, final, *refs):
    got, refs = refs[:n_got], refs[n_got:]
    start, part_share, block, rim, lag_ref, table, inverse, keys, values, bias, taps, w_in, below_core, _ = refs[:14]
    share, short_share, pass_on, spec, total, mixed, proj = refs[14:]
    _, pairs = late_pairs(place, count, got, spec, table)
    accumulate(lag_ref, pairs, True, start, total)
    gated_part(
        place, count, total, inverse, block, rim, keys, values, bias, taps, mixed, proj, w_in, part_share, share,
        short_share,
    )
    if final:
        pass_on[...] = jnp.zeros(pass_on.shape, bf16)
    else:
        pass_half(place, short_share, below_core, pass_on)


def early_first(place, count, block, product, lag_ref, table, total, total_conv, spec):
    rows = block.shape[0]
    spec[...] = dot(table[:, 0:rows], block[...])
    accumulate(lag_ref, [(slot_of(place, 0, count, True), spec)], True, None, total)
    spec[...] = dot(table[...], product[...])
    accumulate(lag_ref, [(slot_of(place, 0, count, False), spec)], False, None, total_conv)


def middle_first(place, count, ms, *refs):
    got, (start, start_conv, lag_ref, table, total, total_conv, spec) = refs[: len(ms)], refs[len(ms) :]
    for i, m in enumerate(ms):
        spec[i] = dot(table[:, 0 : got[i].shape[0]], got[i][...])
    for adjoint, begin, end in ((True, start, total), (False, start_conv, total_conv)):
        pairs = [(slot_of(place, m, count, adjoint), spec.at[i]) for i, m in enumerate(ms)]
        accumulate(lag_ref, pairs, adjoint, begin, end)


def late_first(place, count, n_got, *refs):
    got, refs = refs[:n_got], refs[n_got:]
    start, start_conv, d_out, product, block, rim, lag_ref, table, inverse = refs[:9]
    keys, values, bias, taps, w_in, _ = refs[9:15]
    share, short_share, conv, spec, total, mixed, proj = refs[15:]
    width = 2 * block.shape[1]
    pairs_conv, pairs = late_pairs(place, count, got, spec, table)
    accumulate(lag_ref, pairs_conv, False, start_conv, total)
    whole = dot(inverse[...], total[...]) + bias[0:1, lanes(0, width, place[1])] * product[...].astype(f32)
    conv[...] = whole.astype(bf16)
    query_part(place, count, d_out, conv, taps, mixed, proj)
    share[...] = dot_last(proj[...], w_in[:, lanes(0, width, place[1])])
    accumulate(lag_ref, pairs, True, start, total)
    gated_part(
        place, count, total, inverse, block, rim, keys, values, bias, taps, mixed, proj, w_in, share, share, short_share
    )


def shards(cotangent, projected, w_in, w_out, short_filter, long_filter, filter_bias):
    seq_count = lax.axis_size("seq")
    section_count = lax.axis_size("section")
    seq_place = lax.axis_index("seq")
    section_place = lax.axis_index("section")
    chips = seq_count // 2
    core = seq_place % 2
    own_rows = projected.shape[2]
    rows = 2 * own_rows
    width = w_out.shape[2]
    chans = width // 2
    ext = rows + PAD
    limit = (8 + 3 * chips) * 1024 * 1024
    table, lag_table, inverse = tables(rows)
    weight_in, weight_out, bias = w_in[0], w_out[0], filter_bias
    taps = jnp.transpose(short_filter, (1, 0, 2))

    def swap_core(value):
        return lax.ppermute(value, "seq", [(i, i ^ 1) for i in range(seq_count)])

    def swap_chip(value, m):
        return lax.ppermute(value, "seq", [(i, ((i // 2) ^ m) * 2 + i % 2) for i in range(seq_count)])

    def swap_section(value, upper):
        pairs = []
        for i in range(seq_count):
            for s in range(section_count):
                t = s - 1 if (s - upper) % 2 == 0 else s + 1
                j, t = (i, t) if 0 <= t < section_count else (i ^ 1, s)
                pairs.append((i * section_count + s, j * section_count + t))
        return lax.ppermute(value, ("seq", "section"), pairs)

    def shape(n, kind, across=chans):
        return jax.ShapeDtypeStruct((n, across), kind)

    def run(body, outs, scratch, name, micros, *operands):
        return call(body, outs, scratch, name, limit, micros, *operands)

    stored, grad = projected[0, 0], cotangent[0]
    lags_own, lags_other = run(
        split_lags, [shape(own_rows, bf16), shape(own_rows, bf16)], [], "split_lags", 0.4, long_filter[0]
    )
    stored_other, rim_send = run(
        split_stored, [shape(own_rows, bf16, 3 * chans), shape(PAD, bf16, 4 * width)], [], "split_stored", 0.6,
        stored, grad, lags_other,
    )
    lags_core = swap_core(lags_other)
    rim_pairs = [(2 * q + 1, (2 * q + 2) % seq_count) for q in range(chips)]
    rim_own = lax.ppermute(rim_send, "seq", rim_pairs + [(b, a) for a, b in rim_pairs])
    lags_here = jnp.where(
        core == 0, jnp.concatenate([lags_own, lags_core]), jnp.concatenate([lags_core, lags_own])
    )
    pieces = [lags_here] + [swap_chip(lags_here, m) for m in range(1, chips)]
    stored_core = swap_core(stored_other)
    grad_core = swap_core(grad)
    rim_core = swap_core(rim_own)
    query, keys, values, product, grad = run(
        mix_stored,
        [shape(ext, f32), shape(ext, f32), shape(ext, f32), shape(ext, bf16), shape(own_rows + PAD, bf16, width)],
        [pltpu.VMEM((rows + 2 * PAD, chans), f32)],
        "mix_stored", 1.3,
        stored, stored_core, rim_own, rim_core, grad, taps, pieces[1], pieces[2],
    )
    spectra = run(
        lambda place, *refs: lag_spectra(place, chips, *refs),
        jax.ShapeDtypeStruct((chips + 1, 2 * ext, chans), f32),
        [pltpu.VMEM((chips * rows + ext + PAD, chans), bf16)],
        "lag_spectra", 2.4,
        *pieces, lag_table,
    )

    weight_half = lax.dynamic_slice_in_dim(weight_out, core * chans, chans, 0)
    below = lax.ppermute(
        weight_half, "section", [(s, (s + 1) % section_count) for s in range(section_count)]
    )
    below_core = swap_core(below)

    spec = pltpu.VMEM((2 * ext, chans), f32)
    total_wide = shape(2 * ext, f32)
    total_scratch = pltpu.VMEM((2 * ext, chans), bf16)
    mixed = pltpu.VMEM((ext + PAD, chans), f32)
    ms = list(range(1, chips // 2))
    specs = pltpu.VMEM((len(ms), 2 * ext, chans), f32)
    late_specs = pltpu.VMEM((chips - 1 - len(ms), 2 * ext, chans), f32)
    gates = [shape(rows, bf16), shape(own_rows, bf16), shape(own_rows, bf16), shape(PAD, bf16)]
    proj = pltpu.VMEM((ext, chans), bf16)
    late_outs = [shape(ext, f32, width), shape(ext, bf16, width)]
    ends = [shape(own_rows + PAD, f32, width), shape(own_rows + PAD, bf16, width)]
    result = jnp.zeros((own_rows, width), bf16)
    conv = d_out = ready = None
    for turn in range(section_count):
        first, final = turn == 0, turn == section_count - 1
        upper = section_count - 1 - turn
        if first:
            block, upper_half, lower_half, rim, d_out = run(
                gate_grad, gates + [shape(ext, f32)], [], "gate_grad", 1.0, grad, grad_core, weight_out, query
            )
        else:
            block, upper_half, lower_half, rim = run(gate_only, gates, [], "gate_only", 0.3, d_out, query, ready)

        def send(value, at, m):
            if first:
                value = jnp.where(((seq_place // 2) ^ m) > seq_place // 2, product[at], value)
            return swap_chip(value, m)

        got = [send(block, slice(0, rows), m) for m in range(1, chips - 1)]
        got.append(send(upper_half, slice(0, own_rows), chips - 1))
        got.append(send(lower_half, slice(own_rows, rows), chips - 1))
        soon, last = got[: len(ms)], got[len(ms) :]
        if not first:
            grad_core = swap_core(grad)
        if first:
            start, start_conv = run(
                lambda place, *refs: early_first(place, chips, *refs),
                [total_wide, total_wide], [spec], "early_first", 1.8, block, product, spectra, table,
            )
            carried = run(carry_grad, shape(ext, f32), [], "carry_grad", 1.0, grad, grad_core, below, start)
            start, start_conv = run(
                lambda place, *refs: middle_first(place, chips, ms, *refs),
                [total_wide, total_wide], [specs], "middle_first", 1.0, *soon, start, start_conv, spectra, table,
            )
            share, short_share, conv = run(
                lambda place, *refs: late_first(place, chips, len(last), *refs),
                late_outs + [shape(ext, bf16)], [late_specs, total_scratch, mixed, proj], "late_first", 4.0,
                *last, start, start_conv, d_out, product, block, rim, spectra, table, inverse, keys, values, bias,
                taps, weight_in, carried,
            )
            pass_on = run(pass_half, shape(ext, bf16), [], "pass_half", 0.5, short_share, below_core)
        else:
            start, part_share = run(
                lambda place, *refs: early(place, chips, *refs),
                [total_wide, shape(ext, f32, width)], [spec, mixed, proj], "early", 1.6,
                block, d_out, conv, spectra, table, taps, weight_in,
            )
            start = run(
                lambda place, *refs: middle(place, chips, ms, *refs),
                total_wide, [specs], "middle", 0.8, *soon, start, spectra, table,
            )
            carried = start
            if not final:
                carried = run(carry_grad, shape(ext, f32), [], "carry_grad", 1.0, grad, grad_core, below, start)
            share, short_share, pass_on = run(
                lambda place, *refs, final=final: late(place, chips, len(last), final, *refs),
                late_outs + [shape(ext, bf16)], [late_specs, total_scratch, mixed, proj], "late", 2.5,
                *last, start, part_share, block, rim, spectra, table, inverse, keys, values, bias, taps, weight_in,
                below_core, carried,
            )
        half = pass_on
        if not final:
            keep = run(keep_half, shape(ext, f32), [], "keep_half", 0.6, short_share, below, carried)
            half = (keep + swap_core(pass_on).astype(f32)).astype(bf16)
            d_out = swap_section(half, upper)
        keep_rows, pass_rows = run(split_rows, ends, [], "split_rows", 0.3, share, half)
        ready = (grad.astype(f32) + keep_rows + swap_core(pass_rows).astype(f32)).astype(bf16)
        result = jnp.where(section_place == upper, ready[:own_rows], result)
        if not final:
            grad = swap_section(ready, upper)
    return result[None, None]


def solution(mesh):
    return jax.shard_map(
        shards,
        mesh=mesh,
        in_specs=(
            P(None, "seq", None),
            P("section", None, "seq", None),
            P("section", None, None),
            P("section", None, None),
            P("section", None, None),
            P("section", "seq", None),
            P("section", None),
        ),
        out_specs=P("section", None, "seq", None),
        check_vma=False,
    )
```

```python
import math

import jax
import jax.numpy as jnp
import numpy as np
from jax import lax
from jax.experimental import pallas as pl
from jax.experimental.pallas import tpu as pltpu
from jax.sharding import PartitionSpec as P

f32 = jnp.float32
bf16 = jnp.bfloat16
PAD = 16
CONTRACT = (((1,), (1,)), ((), ()))


def tables(rows):
    period = 2 * rows + 2 * PAD
    half = period // 2
    freq = 2.0 * math.pi * (np.arange(half) + 0.5) / period

    def forward(index):
        angle = np.outer(freq, index)
        return np.concatenate([np.cos(angle), -np.sin(angle)], axis=0)

    series = forward(np.arange(rows + PAD))
    lags = forward(np.arange(period) - (rows + PAD))
    angle = np.outer(np.arange(rows + PAD), freq)
    inverse = np.concatenate([np.cos(angle), -np.sin(angle)], axis=1) * (2.0 / period)
    return tuple(jnp.asarray(t.astype(np.float32), dtype=bf16) for t in (series, lags, inverse))


def dot(a, b):
    return jnp.dot(a, b, preferred_element_type=f32)


def dot_last(a, b):
    return lax.dot_general(a, b, CONTRACT, preferred_element_type=f32)


def lanes(part, width, core):
    half = width // 2
    return pl.ds(pl.multiple_of(part * width + core * half, 128), half)


def side_rows(side, own):
    return pl.ds(pl.multiple_of(side * own, 16), own)


def call(body, outs, scratch, name, limit, micros, *operands):
    vmem = pl.BlockSpec(memory_space=pltpu.VMEM)

    def placed(*refs):
        seq = lax.axis_index("seq")
        body((seq // 2, seq % 2), *refs)

    return pl.pallas_call(
        placed,
        out_shape=outs,
        in_specs=[vmem] * len(operands),
        out_specs=jax.tree.map(lambda _: vmem, outs),
        scratch_shapes=scratch,
        compiler_params=pltpu.CompilerParams(vmem_limit_bytes=limit),
        cost_estimate=pl.CostEstimate(flops=int(micros * 1e9), bytes_accessed=0, transcendentals=0),
        name=name,
    )(*operands)


def split_inputs(place, lags, stored, grad, lags_own, lags_other, other, rim):
    core = place[1]
    rows, chans = lags_own.shape
    width = 2 * chans
    lags_own[...] = lags[:, lanes(0, width, core)].astype(bf16)
    lags_other[...] = lags[:, lanes(0, width, 1 - core)].astype(bf16)
    for part in range(3):
        other[:, part * chans : (part + 1) * chans] = stored[:, lanes(part, width, 1 - core)]
    edge = pl.ds(pl.multiple_of(core * (rows - PAD), 16), PAD)
    rim[:, : 3 * width] = stored[edge]
    rim[:, 3 * width :] = grad[edge]


def mix_stored(place, stored, stored_core, rim_own, rim_core, grad, taps, _, __, query, keys, values, product, grad_ext, padded):
    core = place[1]
    own, width = grad.shape
    rows = 2 * own
    ext = rows + PAD
    for part in range(3):
        at = lanes(part, width, core)
        here = pl.ds(part * (width // 2), width // 2)
        before = jnp.where(core == 0, rim_own[:, at], rim_core[:, at])
        before = jnp.where(place[0] == 0, jnp.zeros_like(before), before)
        after = jnp.where(core == 0, rim_core[:, at], rim_own[:, at])
        padded[0:PAD] = before.astype(f32)
        padded[pl.ds(pl.multiple_of(PAD + core * own, 16), own)] = stored[:, at].astype(f32)
        padded[pl.ds(pl.multiple_of(PAD + (1 - core) * own, 16), own)] = stored_core[:, here].astype(f32)
        padded[PAD + rows : 2 * PAD + rows] = after.astype(f32)
        mixed = (
            taps[0, :, at] * padded[PAD : PAD + ext]
            + taps[1, :, at] * padded[PAD - 1 : PAD - 1 + ext]
            + taps[2, :, at] * padded[PAD - 2 : PAD - 2 + ext]
        )
        (query, keys, values)[part][...] = mixed
    product[...] = (keys[...] * values[...]).astype(bf16)
    grad_ext[0:own] = grad[...]
    grad_ext[own:] = jnp.where(core == 0, rim_core[:, 3 * width :], rim_own[:, 3 * width :])


def lag_spectra(place, count, *refs):
    pieces, (table, out, padded) = refs[:count], refs[count:]
    rows, chans = pieces[0].shape
    chip = place[0]
    ext = rows + PAD
    padded[0:ext] = jnp.zeros((ext, chans), bf16)
    padded[ext + count * rows :] = jnp.zeros((PAD, chans), bf16)
    for m in range(count):
        at = pl.multiple_of(ext + (chip ^ m) * rows, 16)
        padded[pl.ds(at, rows)] = pieces[m][...]
    for d in range(count):
        out[d] = dot(table[...], padded[pl.ds(d * rows, 2 * ext)])
    out[count] = jnp.zeros(out.shape[1:], f32)


def gate_grad(place, g_own, g_core, w_out, query, block, upper, lower, rim, d_out):
    core = place[1]
    rows, chans = block.shape
    own = rows // 2
    weight = w_out[pl.ds(pl.multiple_of(core * chans, 16), chans)]
    wide = dot_last(g_own[...], weight)
    d_out[side_rows(core, own)] = wide[:own]
    d_out[rows:] = wide[own:]
    d_out[side_rows(1 - core, own)] = dot_last(g_core[0:own], weight)
    upper[...] = (d_out[0:own] * query[0:own]).astype(bf16)
    lower[...] = (d_out[own:rows] * query[own:rows]).astype(bf16)
    block[0:own] = upper[...]
    block[own:rows] = lower[...]
    rim[...] = (d_out[rows:] * query[rows:]).astype(bf16)


def gate_only(place, d_out, query, _, block, upper, lower, rim):
    rows = block.shape[0]
    own = rows // 2
    d_conv = (d_out[...].astype(f32) * query[...]).astype(bf16)
    upper[...] = d_conv[0:own]
    lower[...] = d_conv[own:rows]
    block[...] = d_conv[0:rows]
    rim[...] = d_conv[rows:]


def carry_grad(place, g_own, g_core, below, _, out):
    core = place[1]
    rows = out.shape[0] - PAD
    own = rows // 2
    wide = dot_last(g_own[...], below[...])
    out[side_rows(core, own)] = wide[:own]
    out[rows:] = wide[own:]
    out[side_rows(1 - core, own)] = dot_last(g_core[0:own], below[...])


def split_rows(place, share, _, keep, pass_on):
    rows = share.shape[0] - PAD
    own = rows // 2
    keep[0:own] = share[side_rows(place[1], own)]
    keep[own:] = share[rows:]
    pass_on[0:own] = share[side_rows(1 - place[1], own)].astype(bf16)
    pass_on[own:] = share[rows:].astype(bf16)


def keep_half(place, short_share, below, carried, keep):
    keep[...] = carried[...] + dot_last(short_share[...], below[...])


def pass_half(place, short_share, below_core, pass_on):
    pass_on[...] = dot_last(short_share[...], below_core[...]).astype(bf16)


def slot_of(place, m, count, adjoint):
    chip, other = place[0], place[0] ^ m
    distance = other - chip if adjoint else chip - other
    return jnp.where(distance >= 0, distance, count)


def accumulate(lag_ref, pairs, adjoint, start, total):
    step = 16
    half = total.shape[0] // 2

    def tile(i, carry):
        upper = pl.ds(pl.multiple_of(i * step, step), step)
        lower = pl.ds(pl.multiple_of(half + i * step, step), step)
        real, imag = (None, None) if start is None else (start[upper], start[lower])
        for slot, at in pairs:
            lag_re, lag_im = lag_ref[slot, upper], lag_ref[slot, lower]
            if isinstance(at, tuple):
                across = slice(at[1], at[1] + lag_ref.shape[2])
                ser_re, ser_im = at[0][upper, across], at[0][lower, across]
            else:
                ser_re, ser_im = at[upper], at[lower]
            if adjoint:
                re = lag_re * ser_re + lag_im * ser_im
                im = lag_re * ser_im - lag_im * ser_re
            else:
                re = lag_re * ser_re - lag_im * ser_im
                im = lag_re * ser_im + lag_im * ser_re
            real = re if real is None else real + re
            imag = im if imag is None else imag + im
        total[upper] = real.astype(total.dtype)
        total[lower] = imag.astype(total.dtype)
        return carry

    lax.fori_loop(0, half // step, tile, 0)


def short_adjoint(taps, at, mixed, ext):
    mixed[ext:] = jnp.zeros((PAD, mixed.shape[1]), f32)
    return (
        taps[0, :, at] * mixed[0:ext] + taps[1, :, at] * mixed[1 : ext + 1] + taps[2, :, at] * mixed[2 : ext + 2]
    ).astype(bf16)


def inside(place, count):
    return jnp.where(place[0] < count - 1, 1.0, 0.0)


def query_part(place, count, d_out, conv, taps, mixed, proj_query):
    ext, chans = d_out.shape
    rows, width = ext - PAD, 2 * chans
    at = lanes(0, width, place[1])
    mixed[0:ext] = (d_out[...].astype(f32) * conv[...].astype(f32)).astype(bf16).astype(f32)
    mixed[rows:ext] = mixed[rows:ext] * inside(place, count)
    proj_query[...] = short_adjoint(taps, at, mixed, ext)


def gated_part(
    place, count, total, inverse, block, rim, keys, values, bias, taps, mixed, proj, w_in, part_share, share, short_share
):
    core = place[1]
    rows, chans = block.shape
    ext, width = rows + PAD, 2 * chans
    bias_here = bias[0:1, lanes(0, width, core)]
    mixed[0:rows] = bias_here * block[...].astype(f32)
    mixed[rows:ext] = bias_here * rim[...].astype(f32)
    d_prod = (dot(inverse[...], total[...]) + mixed[0:ext]).astype(bf16).astype(f32)
    sums = part_share[...]
    for part, other in ((1, values), (2, keys)):
        at = lanes(part, width, core)
        mixed[0:ext] = (d_prod * other[...]).astype(bf16).astype(f32)
        mixed[rows:ext] = mixed[rows:ext] * inside(place, count)
        proj[...] = short_adjoint(taps, at, mixed, ext)
        sums = sums + dot_last(proj[...], w_in[:, at])
    share[...] = sums
    short_share[...] = sums.astype(bf16)


def early(place, count, block, d_out, conv, lag_ref, table, taps, w_in, total, share, spec, mixed, proj):
    rows = block.shape[0]
    spec[...] = dot(table[:, 0:rows], block[...])
    accumulate(lag_ref, [(slot_of(place, 0, count, True), spec)], True, None, total)
    query_part(place, count, d_out, conv, taps, mixed, proj)
    share[...] = dot_last(proj[...], w_in[:, lanes(0, w_in.shape[0], place[1])])


def middle(place, count, ms, *refs):
    got, (start, lag_ref, table, total, spec) = refs[: len(ms)], refs[len(ms) :]
    pairs = []
    for i, m in enumerate(ms):
        spec[i] = dot(table[:, 0 : got[i].shape[0]], got[i][...])
        pairs.append((slot_of(place, m, count, True), spec.at[i]))
    accumulate(lag_ref, pairs, True, start, total)


def late_pairs(place, count, got, spec, table, side):
    rows, chans = side.shape[0], got[0].shape[1]
    blocks = side.shape[1] // chans
    first = count - blocks
    at = 0
    for i in range(blocks):
        here = slice(i * chans, (i + 1) * chans)
        if got[at].shape[0] == rows:
            side[:, here] = got[at][...]
            at += 1
        else:
            half = rows // 2
            side[0:half, here] = got[at][...]
            side[half:rows, here] = got[at + 1][...]
            at += 2
    spec[...] = dot(table[:, 0:rows], side[...])
    pairs = [(first + i, (spec, i * chans)) for i in range(blocks)]
    return [[(slot_of(place, m, count, adjoint), at) for m, at in pairs] for adjoint in (False, True)]


def late(place, count, n_got, final, *refs):
    got, refs = refs[:n_got], refs[n_got:]
    start, part_share, block, rim, lag_ref, table, inverse, keys, values, bias, taps, w_in, below_core, _ = refs[:14]
    share, short_share, pass_on, spec, total, mixed, proj, side = refs[14:]
    _, pairs = late_pairs(place, count, got, spec, table, side)
    accumulate(lag_ref, pairs, True, start, total)
    gated_part(
        place, count, total, inverse, block, rim, keys, values, bias, taps, mixed, proj, w_in, part_share, share,
        short_share,
    )
    if final:
        pass_on[...] = jnp.zeros(pass_on.shape, bf16)
    else:
        pass_half(place, short_share, below_core, pass_on)


def early_first(place, count, block, product, lag_ref, table, total, total_conv, spec):
    rows = block.shape[0]
    spec[...] = dot(table[:, 0:rows], block[...])
    accumulate(lag_ref, [(slot_of(place, 0, count, True), spec)], True, None, total)
    spec[...] = dot(table[...], product[...])
    accumulate(lag_ref, [(slot_of(place, 0, count, False), spec)], False, None, total_conv)


def middle_first(place, count, ms, *refs):
    got, (start, start_conv, lag_ref, table, total, total_conv, spec) = refs[: len(ms)], refs[len(ms) :]
    for i, m in enumerate(ms):
        spec[i] = dot(table[:, 0 : got[i].shape[0]], got[i][...])
    for adjoint, begin, end in ((True, start, total), (False, start_conv, total_conv)):
        pairs = [(slot_of(place, m, count, adjoint), spec.at[i]) for i, m in enumerate(ms)]
        accumulate(lag_ref, pairs, adjoint, begin, end)


def late_first(place, count, n_got, *refs):
    got, refs = refs[:n_got], refs[n_got:]
    start, start_conv, d_out, product, block, rim, lag_ref, table, inverse = refs[:9]
    keys, values, bias, taps, w_in = refs[9:14]
    share, short_share, conv, spec, total, mixed, proj, side = refs[14:]
    width = 2 * block.shape[1]
    pairs_conv, pairs = late_pairs(place, count, got, spec, table, side)
    accumulate(lag_ref, pairs_conv, False, start_conv, total)
    whole = dot(inverse[...], total[...]) + bias[0:1, lanes(0, width, place[1])] * product[...].astype(f32)
    conv[...] = whole.astype(bf16)
    query_part(place, count, d_out, conv, taps, mixed, proj)
    share[...] = dot_last(proj[...], w_in[:, lanes(0, width, place[1])])
    accumulate(lag_ref, pairs, True, start, total)
    gated_part(
        place, count, total, inverse, block, rim, keys, values, bias, taps, mixed, proj, w_in, share, share, short_share
    )


def shards(cotangent, projected, w_in, w_out, short_filter, long_filter, filter_bias):
    seq_count = lax.axis_size("seq")
    section_count = lax.axis_size("section")
    seq_place = lax.axis_index("seq")
    section_place = lax.axis_index("section")
    chips = seq_count // 2
    core = seq_place % 2
    own_rows = projected.shape[2]
    rows = 2 * own_rows
    width = w_out.shape[2]
    chans = width // 2
    ext = rows + PAD
    limit = (8 + 3 * chips) * 1024 * 1024
    table, lag_table, inverse = tables(rows)
    weight_in, weight_out, bias = w_in[0], w_out[0], filter_bias
    taps = jnp.transpose(short_filter, (1, 0, 2))

    def swap_core(value):
        return lax.ppermute(value, "seq", [(i, i ^ 1) for i in range(seq_count)])

    def swap_chip(value, m):
        return lax.ppermute(value, "seq", [(i, ((i // 2) ^ m) * 2 + i % 2) for i in range(seq_count)])

    def swap_section(value, upper):
        pairs = []
        for i in range(seq_count):
            for s in range(section_count):
                t = s - 1 if (s - upper) % 2 == 0 else s + 1
                j, t = (i, t) if 0 <= t < section_count else (i ^ 1, s)
                pairs.append((i * section_count + s, j * section_count + t))
        return lax.ppermute(value, ("seq", "section"), pairs)

    def shape(n, kind, across=chans):
        return jax.ShapeDtypeStruct((n, across), kind)

    def run(body, outs, scratch, name, micros, *operands):
        return call(body, outs, scratch, name, limit, micros, *operands)

    stored, grad = projected[0, 0], cotangent[0]
    lags_own, lags_other, stored_other, rim_send = call(
        split_inputs,
        [shape(own_rows, bf16), shape(own_rows, bf16), shape(own_rows, bf16, 3 * chans), shape(PAD, bf16, 4 * width)],
        [], "split_inputs", 56 * 1024 * 1024, 1.0, long_filter[0], stored, grad,
    )
    lags_core = swap_core(lags_other)
    rim_pairs = [(2 * q + 1, (2 * q + 2) % seq_count) for q in range(chips)]
    rim_own = lax.ppermute(rim_send, "seq", rim_pairs + [(b, a) for a, b in rim_pairs])
    lags_here = jnp.where(
        core == 0, jnp.concatenate([lags_own, lags_core]), jnp.concatenate([lags_core, lags_own])
    )
    pieces = [lags_here] + [swap_chip(lags_here, m) for m in range(1, chips)]
    stored_core = swap_core(stored_other)
    grad_core = swap_core(grad)
    rim_core = swap_core(rim_own)
    query, keys, values, product, grad = run(
        mix_stored,
        [shape(ext, f32), shape(ext, f32), shape(ext, f32), shape(ext, bf16), shape(own_rows + PAD, bf16, width)],
        [pltpu.VMEM((rows + 2 * PAD, chans), f32)],
        "mix_stored", 1.3,
        stored, stored_core, rim_own, rim_core, grad, taps, pieces[1], pieces[2],
    )
    spectra = run(
        lambda place, *refs: lag_spectra(place, chips, *refs),
        jax.ShapeDtypeStruct((chips + 1, 2 * ext, chans), f32),
        [pltpu.VMEM((chips * rows + ext + PAD, chans), bf16)],
        "lag_spectra", 2.4,
        *pieces, lag_table,
    )

    weight_half = lax.dynamic_slice_in_dim(weight_out, core * chans, chans, 0)
    below = lax.ppermute(
        weight_half, "section", [(s, (s + 1) % section_count) for s in range(section_count)]
    )
    below, _ = lax.optimization_barrier((below, spectra))
    below_core = swap_core(below)

    spec = pltpu.VMEM((2 * ext, chans), f32)
    total_wide = shape(2 * ext, f32)
    total_scratch = pltpu.VMEM((2 * ext, chans), bf16)
    mixed = pltpu.VMEM((ext + PAD, chans), f32)
    ms = list(range(1, chips // 2))
    specs = pltpu.VMEM((len(ms), 2 * ext, chans), f32)
    late_count = chips - 1 - len(ms)
    late_specs = pltpu.VMEM((2 * ext, late_count * chans), f32)
    side = pltpu.VMEM((rows, late_count * chans), bf16)
    gates = [shape(rows, bf16), shape(own_rows, bf16), shape(own_rows, bf16), shape(PAD, bf16)]
    proj = pltpu.VMEM((ext, chans), bf16)
    late_outs = [shape(ext, f32, width), shape(ext, bf16, width)]
    ends = [shape(own_rows + PAD, f32, width), shape(own_rows + PAD, bf16, width)]
    result = jnp.zeros((own_rows, width), bf16)
    conv = d_out = ready = None
    for turn in range(section_count):
        first, final = turn == 0, turn == section_count - 1
        upper = section_count - 1 - turn
        if first:
            block, upper_half, lower_half, rim, d_out = run(
                gate_grad, gates + [shape(ext, f32)], [], "gate_grad", 1.0, grad, grad_core, weight_out, query
            )
        else:
            block, upper_half, lower_half, rim = run(gate_only, gates, [], "gate_only", 0.3, d_out, query, ready)

        def send(value, at, m):
            if first:
                value = jnp.where(((seq_place // 2) ^ m) > seq_place // 2, product[at], value)
            return swap_chip(value, m)

        got = [send(block, slice(0, rows), m) for m in range(1, chips - 1)]
        if first:
            got.append(send(block, slice(0, rows), chips - 1))
        else:
            got.append(send(upper_half, slice(0, own_rows), chips - 1))
            got.append(send(lower_half, slice(own_rows, rows), chips - 1))
        soon, last = got[: len(ms)], got[len(ms) :]
        if not first:
            grad_core = swap_core(grad)
        if first:
            start, start_conv = run(
                lambda place, *refs: early_first(place, chips, *refs),
                [total_wide, total_wide], [spec], "early_first", 1.8, block, product, spectra, table,
            )
            start, start_conv = run(
                lambda place, *refs: middle_first(place, chips, ms, *refs),
                [total_wide, total_wide], [specs], "middle_first", 1.0, *soon, start, start_conv, spectra, table,
            )
            share, short_share, conv = run(
                lambda place, *refs: late_first(place, chips, len(last), *refs),
                late_outs + [shape(ext, bf16)], [late_specs, total_scratch, mixed, proj, side], "late_first", 4.0,
                *last, start, start_conv, d_out, product, block, rim, spectra, table, inverse, keys, values, bias,
                taps, weight_in,
            )
            carried = run(carry_grad, shape(ext, f32), [], "carry_grad", 1.0, grad, grad_core, below, start)
            pass_on = run(pass_half, shape(ext, bf16), [], "pass_half", 0.5, short_share, below_core)
        else:
            start, part_share = run(
                lambda place, *refs: early(place, chips, *refs),
                [total_wide, shape(ext, f32, width)], [spec, mixed, proj], "early", 1.6,
                block, d_out, conv, spectra, table, taps, weight_in,
            )
            start = run(
                lambda place, *refs: middle(place, chips, ms, *refs),
                total_wide, [specs], "middle", 0.8, *soon, start, spectra, table,
            )
            carried = start
            if not final:
                carried = run(carry_grad, shape(ext, f32), [], "carry_grad", 1.0, grad, grad_core, below, start)
            share, short_share, pass_on = run(
                lambda place, *refs, final=final: late(place, chips, len(last), final, *refs),
                late_outs + [shape(ext, bf16)], [late_specs, total_scratch, mixed, proj, side], "late", 2.5,
                *last, start, part_share, block, rim, spectra, table, inverse, keys, values, bias, taps, weight_in,
                below_core, carried,
            )
        half = pass_on
        if not final:
            keep = run(keep_half, shape(ext, f32), [], "keep_half", 0.6, short_share, below, carried)
            half = (keep + swap_core(pass_on).astype(f32)).astype(bf16)
            d_out = swap_section(half, upper)
        keep_rows, pass_rows = run(split_rows, ends, [], "split_rows", 0.3, share, half)
        ready = (grad.astype(f32) + keep_rows + swap_core(pass_rows).astype(f32)).astype(bf16)
        result = jnp.where(section_place == upper, ready[:own_rows], result)
        if not final:
            grad = swap_section(ready, upper)
    return result[None, None]


def solution(mesh):
    return jax.shard_map(
        shards,
        mesh=mesh,
        in_specs=(
            P(None, "seq", None),
            P("section", None, "seq", None),
            P("section", None, None),
            P("section", None, None),
            P("section", None, None),
            P("section", "seq", None),
            P("section", None),
        ),
        out_specs=P("section", None, "seq", None),
        check_vma=False,
    )
```

```python
import math

import jax
import jax.numpy as jnp
import numpy as np
from jax import lax
from jax.experimental import pallas as pl
from jax.experimental.pallas import tpu as pltpu
from jax.sharding import PartitionSpec as P

f32 = jnp.float32
bf16 = jnp.bfloat16
PAD = 16
CONTRACT = (((1,), (1,)), ((), ()))


def tables(rows):
    period = 2 * rows + 2 * PAD
    half = period // 2
    freq = 2.0 * math.pi * (np.arange(half) + 0.5) / period

    def forward(index):
        angle = np.outer(freq, index)
        return np.concatenate([np.cos(angle), -np.sin(angle)], axis=0)

    series = forward(np.arange(rows + PAD))
    lags = forward(np.arange(period) - (rows + PAD))
    angle = np.outer(np.arange(rows + PAD), freq)
    inverse = np.concatenate([np.cos(angle), -np.sin(angle)], axis=1) * (2.0 / period)
    return tuple(jnp.asarray(t.astype(np.float32), dtype=bf16) for t in (series, lags, inverse))


def dot(a, b):
    return jnp.dot(a, b, preferred_element_type=f32)


def dot_last(a, b):
    return lax.dot_general(a, b, CONTRACT, preferred_element_type=f32)


def lanes(part, width, core):
    half = width // 2
    return pl.ds(pl.multiple_of(part * width + core * half, 128), half)


def side_rows(side, own):
    return pl.ds(pl.multiple_of(side * own, 16), own)


def call(body, outs, scratch, name, limit, micros, *operands):
    vmem = pl.BlockSpec(memory_space=pltpu.VMEM)

    def placed(*refs):
        seq = lax.axis_index("seq")
        body((seq // 2, seq % 2), *refs)

    return pl.pallas_call(
        placed,
        out_shape=outs,
        in_specs=[vmem] * len(operands),
        out_specs=jax.tree.map(lambda _: vmem, outs),
        scratch_shapes=scratch,
        compiler_params=pltpu.CompilerParams(vmem_limit_bytes=limit),
        cost_estimate=pl.CostEstimate(flops=int(micros * 1e9), bytes_accessed=0, transcendentals=0),
        name=name,
    )(*operands)


def split_inputs(place, lags, stored, grad, lags_own, lags_other, other, rim):
    core = place[1]
    rows, chans = lags_own.shape
    width = 2 * chans
    lags_own[...] = lags[:, lanes(0, width, core)].astype(bf16)
    lags_other[...] = lags[:, lanes(0, width, 1 - core)].astype(bf16)
    for part in range(3):
        other[:, part * chans : (part + 1) * chans] = stored[:, lanes(part, width, 1 - core)]
    edge = pl.ds(pl.multiple_of(core * (rows - PAD), 16), PAD)
    rim[:, : 3 * width] = stored[edge]
    rim[:, 3 * width :] = grad[edge]


def mix_stored(place, stored, stored_core, rim_own, rim_core, grad, taps, _, __, query, keys, values, product, grad_ext, padded):
    core = place[1]
    own, width = grad.shape
    rows = 2 * own
    ext = rows + PAD
    for part in range(3):
        at = lanes(part, width, core)
        here = pl.ds(part * (width // 2), width // 2)
        before = jnp.where(core == 0, rim_own[:, at], rim_core[:, at])
        before = jnp.where(place[0] == 0, jnp.zeros_like(before), before)
        after = jnp.where(core == 0, rim_core[:, at], rim_own[:, at])
        padded[0:PAD] = before.astype(f32)
        padded[pl.ds(pl.multiple_of(PAD + core * own, 16), own)] = stored[:, at].astype(f32)
        padded[pl.ds(pl.multiple_of(PAD + (1 - core) * own, 16), own)] = stored_core[:, here].astype(f32)
        padded[PAD + rows : 2 * PAD + rows] = after.astype(f32)
        mixed = (
            taps[0, :, at] * padded[PAD : PAD + ext]
            + taps[1, :, at] * padded[PAD - 1 : PAD - 1 + ext]
            + taps[2, :, at] * padded[PAD - 2 : PAD - 2 + ext]
        )
        (query, keys, values)[part][...] = mixed
    product[...] = (keys[...] * values[...]).astype(bf16)
    grad_ext[0:own] = grad[...]
    grad_ext[own:] = jnp.where(core == 0, rim_core[:, 3 * width :], rim_own[:, 3 * width :])


def lag_spectra(place, count, *refs):
    pieces, (table, out, padded) = refs[:count], refs[count:]
    rows, chans = pieces[0].shape
    chip = place[0]
    ext = rows + PAD
    padded[0:ext] = jnp.zeros((ext, chans), bf16)
    padded[ext + count * rows :] = jnp.zeros((PAD, chans), bf16)
    for m in range(count):
        at = pl.multiple_of(ext + (chip ^ m) * rows, 16)
        padded[pl.ds(at, rows)] = pieces[m][...]
    for d in range(count):
        out[d] = dot(table[...], padded[pl.ds(d * rows, 2 * ext)])
    out[count] = jnp.zeros(out.shape[1:], f32)


def gate_grad(place, g_own, g_core, w_out, query, block, upper, lower, rim, d_out):
    core = place[1]
    rows, chans = block.shape
    own = rows // 2
    weight = w_out[pl.ds(pl.multiple_of(core * chans, 16), chans)]
    wide = dot_last(g_own[...], weight)
    d_out[side_rows(core, own)] = wide[:own]
    d_out[rows:] = wide[own:]
    d_out[side_rows(1 - core, own)] = dot_last(g_core[0:own], weight)
    upper[...] = (d_out[0:own] * query[0:own]).astype(bf16)
    lower[...] = (d_out[own:rows] * query[own:rows]).astype(bf16)
    block[0:own] = upper[...]
    block[own:rows] = lower[...]
    rim[...] = (d_out[rows:] * query[rows:]).astype(bf16)


def gate_only(place, d_out, query, _, block, upper, lower, rim):
    rows = block.shape[0]
    own = rows // 2
    d_conv = (d_out[...].astype(f32) * query[...]).astype(bf16)
    upper[...] = d_conv[0:own]
    lower[...] = d_conv[own:rows]
    block[...] = d_conv[0:rows]
    rim[...] = d_conv[rows:]


def carry_grad(place, g_own, g_core, below, _, out):
    core = place[1]
    rows = out.shape[0] - PAD
    own = rows // 2
    wide = dot_last(g_own[...], below[...])
    out[side_rows(core, own)] = wide[:own]
    out[rows:] = wide[own:]
    out[side_rows(1 - core, own)] = dot_last(g_core[0:own], below[...])


def split_rows(place, share, _, keep, pass_on):
    rows = share.shape[0] - PAD
    own = rows // 2
    keep[0:own] = share[side_rows(place[1], own)]
    keep[own:] = share[rows:]
    pass_on[0:own] = share[side_rows(1 - place[1], own)].astype(bf16)
    pass_on[own:] = share[rows:].astype(bf16)


def keep_half(place, short_share, below, carried, keep):
    keep[...] = carried[...] + dot_last(short_share[...], below[...])


def pass_half(place, short_share, below_core, pass_on):
    pass_on[...] = dot_last(short_share[...], below_core[...]).astype(bf16)


def slot_of(place, m, count, adjoint):
    chip, other = place[0], place[0] ^ m
    distance = other - chip if adjoint else chip - other
    return jnp.where(distance >= 0, distance, count)


def accumulate(lag_ref, pairs, adjoint, start, total):
    step = 16
    half = total.shape[0] // 2

    def tile(i, carry):
        upper = pl.ds(pl.multiple_of(i * step, step), step)
        lower = pl.ds(pl.multiple_of(half + i * step, step), step)
        real, imag = (None, None) if start is None else (start[upper], start[lower])
        for slot, at in pairs:
            lag_re, lag_im = lag_ref[slot, upper], lag_ref[slot, lower]
            if isinstance(at, tuple):
                across = slice(at[1], at[1] + lag_ref.shape[2])
                ser_re, ser_im = at[0][upper, across], at[0][lower, across]
            else:
                ser_re, ser_im = at[upper], at[lower]
            if adjoint:
                re = lag_re * ser_re + lag_im * ser_im
                im = lag_re * ser_im - lag_im * ser_re
            else:
                re = lag_re * ser_re - lag_im * ser_im
                im = lag_re * ser_im + lag_im * ser_re
            real = re if real is None else real + re
            imag = im if imag is None else imag + im
        total[upper] = real.astype(total.dtype)
        total[lower] = imag.astype(total.dtype)
        return carry

    lax.fori_loop(0, half // step, tile, 0)


def short_adjoint(taps, at, mixed, ext):
    mixed[ext:] = jnp.zeros((PAD, mixed.shape[1]), f32)
    return (
        taps[0, :, at] * mixed[0:ext] + taps[1, :, at] * mixed[1 : ext + 1] + taps[2, :, at] * mixed[2 : ext + 2]
    ).astype(bf16)


def inside(place, count):
    return jnp.where(place[0] < count - 1, 1.0, 0.0)


def query_part(place, count, d_out, conv, taps, mixed, proj_query):
    ext, chans = d_out.shape
    rows, width = ext - PAD, 2 * chans
    at = lanes(0, width, place[1])
    mixed[0:ext] = (d_out[...].astype(f32) * conv[...].astype(f32)).astype(bf16).astype(f32)
    mixed[rows:ext] = mixed[rows:ext] * inside(place, count)
    proj_query[:, 0:chans] = short_adjoint(taps, at, mixed, ext)


def gated_part(
    place, count, total, inverse, block, rim, keys, values, bias, taps, mixed, proj, w_in, part_share, share, short_share
):
    core = place[1]
    rows, chans = block.shape
    ext, width = rows + PAD, 2 * chans
    bias_here = bias[0:1, lanes(0, width, core)]
    mixed[0:rows] = bias_here * block[...].astype(f32)
    mixed[rows:ext] = bias_here * rim[...].astype(f32)
    d_prod = (dot(inverse[...], total[...]) + mixed[0:ext]).astype(bf16).astype(f32)
    for part, other in ((1, values), (2, keys)):
        at = lanes(part, width, core)
        mixed[0:ext] = (d_prod * other[...]).astype(bf16).astype(f32)
        mixed[rows:ext] = mixed[rows:ext] * inside(place, count)
        proj[:, (part - 1) * chans : part * chans] = short_adjoint(taps, at, mixed, ext)
    sums = part_share[...] + dot_last(proj[...], w_in[:, chans:])
    share[...] = sums
    short_share[...] = sums.astype(bf16)


def early(place, count, block, d_out, conv, lag_ref, table, taps, w_in, total, share, spec, mixed, proj):
    rows = block.shape[0]
    spec[...] = dot(table[:, 0:rows], block[...])
    accumulate(lag_ref, [(slot_of(place, 0, count, True), spec)], True, None, total)
    query_part(place, count, d_out, conv, taps, mixed, proj)
    share[...] = dot_last(proj[:, 0 : conv.shape[1]], w_in[:, 0 : conv.shape[1]])


def middle(place, count, ms, *refs):
    got, (start, lag_ref, table, total, spec) = refs[: len(ms)], refs[len(ms) :]
    pairs = []
    for i, m in enumerate(ms):
        spec[i] = dot(table[:, 0 : got[i].shape[0]], got[i][...])
        pairs.append((slot_of(place, m, count, True), spec.at[i]))
    accumulate(lag_ref, pairs, True, start, total)


def late_pairs(place, count, got, spec, table, side):
    rows, chans = side.shape[0], got[0].shape[1]
    blocks = side.shape[1] // chans
    first = count - blocks
    at = 0
    for i in range(blocks):
        here = slice(i * chans, (i + 1) * chans)
        if got[at].shape[0] == rows:
            side[:, here] = got[at][...]
            at += 1
        else:
            half = rows // 2
            side[0:half, here] = got[at][...]
            side[half:rows, here] = got[at + 1][...]
            at += 2
    spec[...] = dot(table[:, 0:rows], side[...])
    pairs = [(first + i, (spec, i * chans)) for i in range(blocks)]
    return [[(slot_of(place, m, count, adjoint), at) for m, at in pairs] for adjoint in (False, True)]


def late(place, count, n_got, final, *refs):
    got, refs = refs[:n_got], refs[n_got:]
    start, part_share, block, rim, lag_ref, table, inverse, keys, values, bias, taps, w_in, below_core = refs[:13]
    share, short_share, pass_on, spec, total, mixed, proj, side = refs[13:]
    _, pairs = late_pairs(place, count, got, spec, table, side)
    accumulate(lag_ref, pairs, True, start, total)
    gated_part(
        place, count, total, inverse, block, rim, keys, values, bias, taps, mixed, proj, w_in, part_share, share,
        short_share,
    )
    if final:
        pass_on[...] = jnp.zeros(pass_on.shape, bf16)
    else:
        pass_half(place, short_share, below_core, pass_on)


def early_first(place, count, block, product, lag_ref, table, w_in, total, total_conv, weight, spec):
    chans = block.shape[1]
    for part in range(3):
        weight[:, part * chans : (part + 1) * chans] = w_in[:, lanes(part, 2 * chans, place[1])]
    rows = block.shape[0]
    spec[...] = dot(table[:, 0:rows], block[...])
    accumulate(lag_ref, [(slot_of(place, 0, count, True), spec)], True, None, total)
    spec[...] = dot(table[...], product[...])
    accumulate(lag_ref, [(slot_of(place, 0, count, False), spec)], False, None, total_conv)


def middle_first(place, count, ms, *refs):
    got, (start, start_conv, lag_ref, table, total, total_conv, spec) = refs[: len(ms)], refs[len(ms) :]
    for i, m in enumerate(ms):
        spec[i] = dot(table[:, 0 : got[i].shape[0]], got[i][...])
    for adjoint, begin, end in ((True, start, total), (False, start_conv, total_conv)):
        pairs = [(slot_of(place, m, count, adjoint), spec.at[i]) for i, m in enumerate(ms)]
        accumulate(lag_ref, pairs, adjoint, begin, end)


def late_first(place, count, n_got, *refs):
    got, refs = refs[:n_got], refs[n_got:]
    start, start_conv, d_out, product, block, rim, lag_ref, table, inverse = refs[:9]
    keys, values, bias, taps, w_in = refs[9:14]
    share, short_share, conv, spec, total, mixed, proj, side = refs[14:]
    width = 2 * block.shape[1]
    pairs_conv, pairs = late_pairs(place, count, got, spec, table, side)
    accumulate(lag_ref, pairs_conv, False, start_conv, total)
    whole = dot(inverse[...], total[...]) + bias[0:1, lanes(0, width, place[1])] * product[...].astype(f32)
    conv[...] = whole.astype(bf16)
    query_part(place, count, d_out, conv, taps, mixed, proj)
    share[...] = dot_last(proj[:, 0 : conv.shape[1]], w_in[:, 0 : conv.shape[1]])
    accumulate(lag_ref, pairs, True, start, total)
    gated_part(
        place, count, total, inverse, block, rim, keys, values, bias, taps, mixed, proj, w_in, share, share, short_share
    )


def shards(cotangent, projected, w_in, w_out, short_filter, long_filter, filter_bias):
    seq_count = lax.axis_size("seq")
    section_count = lax.axis_size("section")
    seq_place = lax.axis_index("seq")
    section_place = lax.axis_index("section")
    chips = seq_count // 2
    core = seq_place % 2
    own_rows = projected.shape[2]
    rows = 2 * own_rows
    width = w_out.shape[2]
    chans = width // 2
    ext = rows + PAD
    limit = (8 + 3 * chips) * 1024 * 1024
    table, lag_table, inverse = tables(rows)
    weight_in, weight_out, bias = w_in[0], w_out[0], filter_bias
    taps = jnp.transpose(short_filter, (1, 0, 2))

    def swap_core(value):
        return lax.ppermute(value, "seq", [(i, i ^ 1) for i in range(seq_count)])

    def swap_chip(value, m):
        return lax.ppermute(value, "seq", [(i, ((i // 2) ^ m) * 2 + i % 2) for i in range(seq_count)])

    def swap_section(value, upper):
        pairs = []
        for i in range(seq_count):
            for s in range(section_count):
                t = s - 1 if (s - upper) % 2 == 0 else s + 1
                j, t = (i, t) if 0 <= t < section_count else (i ^ 1, s)
                pairs.append((i * section_count + s, j * section_count + t))
        return lax.ppermute(value, ("seq", "section"), pairs)

    def shape(n, kind, across=chans):
        return jax.ShapeDtypeStruct((n, across), kind)

    def run(body, outs, scratch, name, micros, *operands):
        return call(body, outs, scratch, name, limit, micros, *operands)

    stored, grad = projected[0, 0], cotangent[0]
    lags_own, lags_other, stored_other, rim_send = call(
        split_inputs,
        [shape(own_rows, bf16), shape(own_rows, bf16), shape(own_rows, bf16, 3 * chans), shape(PAD, bf16, 4 * width)],
        [], "split_inputs", 56 * 1024 * 1024, 1.0, long_filter[0], stored, grad,
    )
    lags_core = swap_core(lags_other)
    rim_pairs = [(2 * q + 1, (2 * q + 2) % seq_count) for q in range(chips)]
    rim_own = lax.ppermute(rim_send, "seq", rim_pairs + [(b, a) for a, b in rim_pairs])
    lags_here = jnp.where(
        core == 0, jnp.concatenate([lags_own, lags_core]), jnp.concatenate([lags_core, lags_own])
    )
    pieces = [lags_here] + [swap_chip(lags_here, m) for m in range(1, chips)]
    stored_core = swap_core(stored_other)
    grad_core = swap_core(grad)
    rim_core = swap_core(rim_own)
    query, keys, values, product, grad = run(
        mix_stored,
        [shape(ext, f32), shape(ext, f32), shape(ext, f32), shape(ext, bf16), shape(own_rows + PAD, bf16, width)],
        [pltpu.VMEM((rows + 2 * PAD, chans), f32)],
        "mix_stored", 1.3,
        stored, stored_core, rim_own, rim_core, grad, taps, pieces[1], pieces[2],
    )
    spectra = run(
        lambda place, *refs: lag_spectra(place, chips, *refs),
        jax.ShapeDtypeStruct((chips + 1, 2 * ext, chans), f32),
        [pltpu.VMEM((chips * rows + ext + PAD, chans), bf16)],
        "lag_spectra", 10.0,
        *pieces, lag_table,
    )

    weight_half = lax.dynamic_slice_in_dim(weight_out, core * chans, chans, 0)
    below = lax.ppermute(
        weight_half, "section", [(s, (s + 1) % section_count) for s in range(section_count)]
    )
    below, _ = lax.optimization_barrier((below, spectra))
    below_core = swap_core(below)

    spec = pltpu.VMEM((2 * ext, chans), f32)
    total_wide = shape(2 * ext, f32)
    total_scratch = pltpu.VMEM((2 * ext, chans), bf16)
    mixed = pltpu.VMEM((ext + PAD, chans), f32)
    ms = list(range(1, chips // 2))
    specs = pltpu.VMEM((len(ms), 2 * ext, chans), f32)
    late_count = chips - 1 - len(ms)
    late_specs = pltpu.VMEM((2 * ext, late_count * chans), f32)
    side = pltpu.VMEM((rows, late_count * chans), bf16)
    gates = [shape(rows, bf16), shape(own_rows, bf16), shape(own_rows, bf16), shape(PAD, bf16)]
    proj = pltpu.VMEM((ext, 2 * chans), bf16)
    late_outs = [shape(ext, f32, width), shape(ext, bf16, width)]
    ends = [shape(own_rows + PAD, f32, width), shape(own_rows + PAD, bf16, width)]
    result = jnp.zeros((own_rows, width), bf16)
    conv = d_out = ready = None
    for turn in range(section_count):
        first, final = turn == 0, turn == section_count - 1
        upper = section_count - 1 - turn
        if first:
            block, upper_half, lower_half, rim, d_out = run(
                gate_grad, gates + [shape(ext, f32)], [], "gate_grad", 1.0, grad, grad_core, weight_out, query
            )
        else:
            block, upper_half, lower_half, rim = run(gate_only, gates, [], "gate_only", 0.3, d_out, query, ready)

        def send(value, at, m):
            if first:
                value = jnp.where(((seq_place // 2) ^ m) > seq_place // 2, product[at], value)
            return swap_chip(value, m)

        got = [send(block, slice(0, rows), m) for m in range(1, chips - 1)]
        if first:
            got.append(send(block, slice(0, rows), chips - 1))
        else:
            got.append(send(upper_half, slice(0, own_rows), chips - 1))
            got.append(send(lower_half, slice(own_rows, rows), chips - 1))
        soon, last = got[: len(ms)], got[len(ms) :]
        if not first:
            grad_core = swap_core(grad)
        if first:
            start, start_conv, weight_own = run(
                lambda place, *refs: early_first(place, chips, *refs),
                [total_wide, total_wide, shape(width, bf16, 3 * chans)], [spec], "early_first", 10.0, block, product, spectra, table, weight_in,
            )
            start, start_conv = run(
                lambda place, *refs: middle_first(place, chips, ms, *refs),
                [total_wide, total_wide], [specs], "middle_first", 10.0, *soon, start, start_conv, spectra, table,
            )
            share, short_share, conv = run(
                lambda place, *refs: late_first(place, chips, len(last), *refs),
                late_outs + [shape(ext, bf16)], [late_specs, total_scratch, mixed, proj, side], "late_first", 4.0,
                *last, start, start_conv, d_out, product, block, rim, spectra, table, inverse, keys, values, bias,
                taps, weight_own,
            )
            carried = run(carry_grad, shape(ext, f32), [], "carry_grad", 1.0, grad, grad_core, below, start)
            pass_on = run(pass_half, shape(ext, bf16), [], "pass_half", 0.5, short_share, below_core)
        else:
            start, part_share = run(
                lambda place, *refs: early(place, chips, *refs),
                [total_wide, shape(ext, f32, width)], [spec, mixed, proj], "early", 1.6,
                block, d_out, conv, spectra, table, taps, weight_own,
            )
            start = run(
                lambda place, *refs: middle(place, chips, ms, *refs),
                total_wide, [specs], "middle", 0.8, *soon, start, spectra, table,
            )
            share, short_share, pass_on = run(
                lambda place, *refs, final=final: late(place, chips, len(last), final, *refs),
                late_outs + [shape(ext, bf16)], [late_specs, total_scratch, mixed, proj, side], "late", 2.5,
                *last, start, part_share, block, rim, spectra, table, inverse, keys, values, bias, taps, weight_own,
                below_core,
            )
            if not final:
                carried = run(carry_grad, shape(ext, f32), [], "carry_grad", 0.5, grad, grad_core, below, pass_on)
        half = pass_on
        if not final:
            keep = run(keep_half, shape(ext, f32), [], "keep_half", 0.6, short_share, below, carried)
            half = (keep + swap_core(pass_on).astype(f32)).astype(bf16)
            d_out = swap_section(half, upper)
        keep_rows, pass_rows = run(split_rows, ends, [], "split_rows", 0.3, share, half)
        ready = (grad.astype(f32) + keep_rows + swap_core(pass_rows).astype(f32)).astype(bf16)
        result = jnp.where(section_place == upper, ready[:own_rows], result)
        if not final:
            grad = swap_section(ready, upper)
    return result[None, None]


def solution(mesh):
    return jax.shard_map(
        shards,
        mesh=mesh,
        in_specs=(
            P(None, "seq", None),
            P("section", None, "seq", None),
            P("section", None, None),
            P("section", None, None),
            P("section", None, None),
            P("section", "seq", None),
            P("section", None),
        ),
        out_specs=P("section", None, "seq", None),
        check_vma=False,
    )
```

```python
import math

import jax
import jax.numpy as jnp
import numpy as np
from jax import lax
from jax.experimental import pallas as pl
from jax.experimental.pallas import tpu as pltpu
from jax.sharding import PartitionSpec as P

f32 = jnp.float32
bf16 = jnp.bfloat16
PAD = 16
CONTRACT = (((1,), (1,)), ((), ()))


def tables(rows):
    period = 2 * rows + 2 * PAD
    half = period // 2
    freq = 2.0 * math.pi * (np.arange(half) + 0.5) / period

    def forward(index):
        angle = np.outer(freq, index)
        return np.concatenate([np.cos(angle), -np.sin(angle)], axis=0)

    series = forward(np.arange(rows + PAD))
    lags = forward(np.arange(period) - (rows + PAD))
    angle = np.outer(np.arange(rows + PAD), freq)
    inverse = np.concatenate([np.cos(angle), -np.sin(angle)], axis=1) * (2.0 / period)
    return tuple(jnp.asarray(t.astype(np.float32), dtype=bf16) for t in (series, lags, inverse))


def dot(a, b):
    return jnp.dot(a, b, preferred_element_type=f32)


def dot_last(a, b):
    return lax.dot_general(a, b, CONTRACT, preferred_element_type=f32)


def lanes(part, width, core):
    half = width // 2
    return pl.ds(pl.multiple_of(part * width + core * half, 128), half)


def side_rows(side, own):
    return pl.ds(pl.multiple_of(side * own, 16), own)


def call(body, outs, scratch, name, limit, micros, *operands):
    vmem = pl.BlockSpec(memory_space=pltpu.VMEM)

    def placed(*refs):
        seq = lax.axis_index("seq")
        body((seq // 2, seq % 2), *refs)

    return pl.pallas_call(
        placed,
        out_shape=outs,
        in_specs=[vmem] * len(operands),
        out_specs=jax.tree.map(lambda _: vmem, outs),
        scratch_shapes=scratch,
        compiler_params=pltpu.CompilerParams(vmem_limit_bytes=limit),
        cost_estimate=pl.CostEstimate(flops=int(micros * 1e9), bytes_accessed=0, transcendentals=0),
        name=name,
    )(*operands)


def split_inputs(place, lags, stored, grad, lags_own, lags_other, other, rim):
    core = place[1]
    rows, chans = lags_own.shape
    width = 2 * chans
    lags_own[...] = lags[:, lanes(0, width, core)].astype(bf16)
    lags_other[...] = lags[:, lanes(0, width, 1 - core)].astype(bf16)
    for part in range(3):
        other[:, part * chans : (part + 1) * chans] = stored[:, lanes(part, width, 1 - core)]
    edge = pl.ds(pl.multiple_of(core * (rows - PAD), 16), PAD)
    rim[:, : 3 * width] = stored[edge]
    rim[:, 3 * width :] = grad[edge]


def mix_stored(place, stored, stored_core, rim_own, rim_core, grad, taps, _, __, ___, query, keys, values, product, grad_ext, padded):
    core = place[1]
    own, width = grad.shape
    rows = 2 * own
    ext = rows + PAD
    for part in range(3):
        at = lanes(part, width, core)
        here = pl.ds(part * (width // 2), width // 2)
        before = jnp.where(core == 0, rim_own[:, at], rim_core[:, at])
        before = jnp.where(place[0] == 0, jnp.zeros_like(before), before)
        after = jnp.where(core == 0, rim_core[:, at], rim_own[:, at])
        padded[0:PAD] = before.astype(f32)
        padded[pl.ds(pl.multiple_of(PAD + core * own, 16), own)] = stored[:, at].astype(f32)
        padded[pl.ds(pl.multiple_of(PAD + (1 - core) * own, 16), own)] = stored_core[:, here].astype(f32)
        padded[PAD + rows : 2 * PAD + rows] = after.astype(f32)
        mixed = (
            taps[0, :, at] * padded[PAD : PAD + ext]
            + taps[1, :, at] * padded[PAD - 1 : PAD - 1 + ext]
            + taps[2, :, at] * padded[PAD - 2 : PAD - 2 + ext]
        )
        (query, keys, values)[part][...] = mixed
    product[...] = (keys[...] * values[...]).astype(bf16)
    grad_ext[0:own] = grad[...]
    grad_ext[own:] = jnp.where(core == 0, rim_core[:, 3 * width :], rim_own[:, 3 * width :])


def lag_spectra(place, count, *refs):
    pieces, (table, out, padded) = refs[:count], refs[count:]
    rows, chans = pieces[0].shape
    chip = place[0]
    ext = rows + PAD
    padded[0:ext] = jnp.zeros((ext, chans), bf16)
    padded[ext + count * rows :] = jnp.zeros((PAD, chans), bf16)
    for m in range(count):
        at = pl.multiple_of(ext + (chip ^ m) * rows, 16)
        padded[pl.ds(at, rows)] = pieces[m][...]
    for d in range(count):
        out[d] = dot(table[...], padded[pl.ds(d * rows, 2 * ext)])
    out[count] = jnp.zeros(out.shape[1:], f32)


def gate_grad(place, g_own, g_core, w_out, query, block, rim, d_out):
    core = place[1]
    rows, chans = block.shape
    own = rows // 2
    weight = w_out[pl.ds(pl.multiple_of(core * chans, 16), chans)]
    wide = dot_last(g_own[...], weight)
    d_out[side_rows(core, own)] = wide[:own]
    d_out[rows:] = wide[own:]
    d_out[side_rows(1 - core, own)] = dot_last(g_core[0:own], weight)
    block[...] = (d_out[0:rows] * query[0:rows]).astype(bf16)
    rim[...] = (d_out[rows:] * query[rows:]).astype(bf16)


def gate_only(place, d_out, query, _, block, upper, lower, rim):
    rows = block.shape[0]
    own = rows // 2
    d_conv = (d_out[...].astype(f32) * query[...]).astype(bf16)
    upper[...] = d_conv[0:own]
    lower[...] = d_conv[own:rows]
    block[...] = d_conv[0:rows]
    rim[...] = d_conv[rows:]


def carry_grad(place, g_own, g_core, below, _, out):
    core = place[1]
    rows = out.shape[0] - PAD
    own = rows // 2
    wide = dot_last(g_own[...], below[...])
    out[side_rows(core, own)] = wide[:own]
    out[rows:] = wide[own:]
    out[side_rows(1 - core, own)] = dot_last(g_core[0:own], below[...])


def split_rows(place, share, _, keep, pass_on):
    rows = share.shape[0] - PAD
    own = rows // 2
    keep[0:own] = share[side_rows(place[1], own)]
    keep[own:] = share[rows:]
    pass_on[0:own] = share[side_rows(1 - place[1], own)].astype(bf16)
    pass_on[own:] = share[rows:].astype(bf16)


def keep_half(place, short_share, below, carried, keep):
    keep[...] = carried[...] + dot_last(short_share[...], below[...])


def pass_half(place, short_share, below_core, pass_on):
    pass_on[...] = dot_last(short_share[...], below_core[...]).astype(bf16)


def slot_of(place, m, count, adjoint):
    chip, other = place[0], place[0] ^ m
    distance = other - chip if adjoint else chip - other
    return jnp.where(distance >= 0, distance, count)


def accumulate(lag_ref, pairs, adjoint, start, total):
    step = 16
    half = total.shape[0] // 2

    def tile(i, carry):
        upper = pl.ds(pl.multiple_of(i * step, step), step)
        lower = pl.ds(pl.multiple_of(half + i * step, step), step)
        real, imag = (None, None) if start is None else (start[upper], start[lower])
        for slot, at in pairs:
            lag_re, lag_im = lag_ref[slot, upper], lag_ref[slot, lower]
            if isinstance(at, tuple):
                across = slice(at[1], at[1] + lag_ref.shape[2])
                ser_re, ser_im = at[0][upper, across], at[0][lower, across]
            else:
                ser_re, ser_im = at[upper], at[lower]
            if adjoint:
                re = lag_re * ser_re + lag_im * ser_im
                im = lag_re * ser_im - lag_im * ser_re
            else:
                re = lag_re * ser_re - lag_im * ser_im
                im = lag_re * ser_im + lag_im * ser_re
            real = re if real is None else real + re
            imag = im if imag is None else imag + im
        total[upper] = real.astype(total.dtype)
        total[lower] = imag.astype(total.dtype)
        return carry

    lax.fori_loop(0, half // step, tile, 0)


def short_adjoint(taps, at, mixed, ext):
    mixed[ext:] = jnp.zeros((PAD, mixed.shape[1]), f32)
    return (
        taps[0, :, at] * mixed[0:ext] + taps[1, :, at] * mixed[1 : ext + 1] + taps[2, :, at] * mixed[2 : ext + 2]
    ).astype(bf16)


def inside(place, count):
    return jnp.where(place[0] < count - 1, 1.0, 0.0)


def query_part(place, count, d_out, conv, taps, mixed, proj_query):
    ext, chans = d_out.shape
    rows, width = ext - PAD, 2 * chans
    at = lanes(0, width, place[1])
    mixed[0:ext] = (d_out[...].astype(f32) * conv[...].astype(f32)).astype(bf16).astype(f32)
    mixed[rows:ext] = mixed[rows:ext] * inside(place, count)
    proj_query[:, 0:chans] = short_adjoint(taps, at, mixed, ext)


def gated_part(
    place, count, total, inverse, block, rim, keys, values, bias, taps, mixed, proj, w_in, part_share, share, short_share
):
    core = place[1]
    rows, chans = block.shape
    ext, width = rows + PAD, 2 * chans
    bias_here = bias[0:1, lanes(0, width, core)]
    mixed[0:rows] = bias_here * block[...].astype(f32)
    mixed[rows:ext] = bias_here * rim[...].astype(f32)
    d_prod = (dot(inverse[...], total[...]) + mixed[0:ext]).astype(bf16).astype(f32)
    for part, other in ((1, values), (2, keys)):
        at = lanes(part, width, core)
        mixed[0:ext] = (d_prod * other[...]).astype(bf16).astype(f32)
        mixed[rows:ext] = mixed[rows:ext] * inside(place, count)
        proj[:, (part - 1) * chans : part * chans] = short_adjoint(taps, at, mixed, ext)
    sums = part_share[...] + dot_last(proj[...], w_in[:, chans:])
    share[...] = sums
    short_share[...] = sums.astype(bf16)


def early(place, count, block, d_out, conv, lag_ref, table, taps, w_in, total, share, spec, mixed, proj):
    rows = block.shape[0]
    spec[...] = dot(table[:, 0:rows], block[...])
    accumulate(lag_ref, [(slot_of(place, 0, count, True), spec)], True, None, total)
    query_part(place, count, d_out, conv, taps, mixed, proj)
    share[...] = dot_last(proj[:, 0 : conv.shape[1]], w_in[:, 0 : conv.shape[1]])


def middle(place, count, ms, *refs):
    got, (start, lag_ref, table, total, spec) = refs[: len(ms)], refs[len(ms) :]
    pairs = []
    for i, m in enumerate(ms):
        spec[i] = dot(table[:, 0 : got[i].shape[0]], got[i][...])
        pairs.append((slot_of(place, m, count, True), spec.at[i]))
    accumulate(lag_ref, pairs, True, start, total)


def late_pairs(place, count, got, spec, table, side):
    rows, chans = side.shape[0], got[0].shape[1]
    blocks = side.shape[1] // chans
    first = count - blocks
    at = 0
    for i in range(blocks):
        here = slice(i * chans, (i + 1) * chans)
        if got[at].shape[0] == rows:
            side[:, here] = got[at][...]
            at += 1
        else:
            half = rows // 2
            side[0:half, here] = got[at][...]
            side[half:rows, here] = got[at + 1][...]
            at += 2
    spec[...] = dot(table[:, 0:rows], side[...])
    pairs = [(first + i, (spec, i * chans)) for i in range(blocks)]
    return [[(slot_of(place, m, count, adjoint), at) for m, at in pairs] for adjoint in (False, True)]


def late(place, count, n_got, final, *refs):
    got, refs = refs[:n_got], refs[n_got:]
    start, part_share, block, rim, lag_ref, table, inverse, keys, values, bias, taps, w_in, below_core = refs[:13]
    if final:
        share, spec, total, mixed, proj, side, short_share = refs[13:]
    else:
        share, short_share, pass_on, spec, total, mixed, proj, side = refs[13:]
    _, pairs = late_pairs(place, count, got, spec, table, side)
    accumulate(lag_ref, pairs, True, start, total)
    gated_part(
        place, count, total, inverse, block, rim, keys, values, bias, taps, mixed, proj, w_in, part_share, share,
        short_share,
    )
    if not final:
        pass_half(place, short_share, below_core, pass_on)


def early_first(place, count, block, product, lag_ref, table, w_in, total, total_conv, weight, spec):
    chans = block.shape[1]
    for part in range(3):
        weight[:, part * chans : (part + 1) * chans] = w_in[:, lanes(part, 2 * chans, place[1])]
    rows = block.shape[0]
    spec[...] = dot(table[:, 0:rows], block[...])
    accumulate(lag_ref, [(slot_of(place, 0, count, True), spec)], True, None, total)
    spec[...] = dot(table[...], product[...])
    accumulate(lag_ref, [(slot_of(place, 0, count, False), spec)], False, None, total_conv)


def middle_first(place, count, ms, *refs):
    got, (start, start_conv, lag_ref, table, total, total_conv, spec) = refs[: len(ms)], refs[len(ms) :]
    for i, m in enumerate(ms):
        spec[i] = dot(table[:, 0 : got[i].shape[0]], got[i][...])
    for adjoint, begin, end in ((True, start, total), (False, start_conv, total_conv)):
        pairs = [(slot_of(place, m, count, adjoint), spec.at[i]) for i, m in enumerate(ms)]
        accumulate(lag_ref, pairs, adjoint, begin, end)


def late_first(place, count, n_got, *refs):
    got, refs = refs[:n_got], refs[n_got:]
    start, start_conv, d_out, product, block, rim, lag_ref, table, inverse = refs[:9]
    keys, values, bias, taps, w_in = refs[9:14]
    share, short_share, conv, spec, total, mixed, proj, side = refs[14:]
    width = 2 * block.shape[1]
    pairs_conv, pairs = late_pairs(place, count, got, spec, table, side)
    accumulate(lag_ref, pairs_conv, False, start_conv, total)
    whole = dot(inverse[...], total[...]) + bias[0:1, lanes(0, width, place[1])] * product[...].astype(f32)
    conv[...] = whole.astype(bf16)
    query_part(place, count, d_out, conv, taps, mixed, proj)
    share[...] = dot_last(proj[:, 0 : conv.shape[1]], w_in[:, 0 : conv.shape[1]])
    accumulate(lag_ref, pairs, True, start, total)
    gated_part(
        place, count, total, inverse, block, rim, keys, values, bias, taps, mixed, proj, w_in, share, share, short_share
    )


def shards(cotangent, projected, w_in, w_out, short_filter, long_filter, filter_bias):
    seq_count = lax.axis_size("seq")
    section_count = lax.axis_size("section")
    seq_place = lax.axis_index("seq")
    section_place = lax.axis_index("section")
    chips = seq_count // 2
    core = seq_place % 2
    own_rows = projected.shape[2]
    rows = 2 * own_rows
    width = w_out.shape[2]
    chans = width // 2
    ext = rows + PAD
    limit = (8 + 3 * chips) * 1024 * 1024
    table, lag_table, inverse = tables(rows)
    weight_in, weight_out, bias = w_in[0], w_out[0], filter_bias
    taps = jnp.transpose(short_filter, (1, 0, 2))

    def swap_core(value):
        return lax.ppermute(value, "seq", [(i, i ^ 1) for i in range(seq_count)])

    def swap_chip(value, m):
        return lax.ppermute(value, "seq", [(i, ((i // 2) ^ m) * 2 + i % 2) for i in range(seq_count)])

    def swap_section(value, upper):
        pairs = []
        for i in range(seq_count):
            for s in range(section_count):
                t = s - 1 if (s - upper) % 2 == 0 else s + 1
                j, t = (i, t) if 0 <= t < section_count else (i ^ 1, s)
                pairs.append((i * section_count + s, j * section_count + t))
        return lax.ppermute(value, ("seq", "section"), pairs)

    def shape(n, kind, across=chans):
        return jax.ShapeDtypeStruct((n, across), kind)

    def run(body, outs, scratch, name, micros, *operands):
        return call(body, outs, scratch, name, limit, micros, *operands)

    stored, grad = projected[0, 0], cotangent[0]
    lags_own, lags_other, stored_other, rim_send = call(
        split_inputs,
        [shape(own_rows, bf16), shape(own_rows, bf16), shape(own_rows, bf16, 3 * chans), shape(PAD, bf16, 4 * width)],
        [], "split_inputs", 56 * 1024 * 1024, 1.0, long_filter[0], stored, grad,
    )
    lags_core = swap_core(lags_other)
    rim_pairs = [(2 * q + 1, (2 * q + 2) % seq_count) for q in range(chips)]
    rim_own = lax.ppermute(rim_send, "seq", rim_pairs + [(b, a) for a, b in rim_pairs])
    lags_here = jnp.where(
        core == 0, jnp.concatenate([lags_own, lags_core]), jnp.concatenate([lags_core, lags_own])
    )
    pieces = [lags_here] + [swap_chip(lags_here, m) for m in range(1, chips)]
    stored_core = swap_core(stored_other)
    grad_core = swap_core(grad)
    rim_core = swap_core(rim_own)
    query, keys, values, product, grad = run(
        mix_stored,
        [shape(ext, f32), shape(ext, f32), shape(ext, f32), shape(ext, bf16), shape(own_rows + PAD, bf16, width)],
        [pltpu.VMEM((rows + 2 * PAD, chans), f32)],
        "mix_stored", 1.3,
        stored, stored_core, rim_own, rim_core, grad, taps, pieces[1], pieces[2], weight_out,
    )
    spectra = run(
        lambda place, *refs: lag_spectra(place, chips, *refs),
        jax.ShapeDtypeStruct((chips + 1, 2 * ext, chans), f32),
        [pltpu.VMEM((chips * rows + ext + PAD, chans), bf16)],
        "lag_spectra", 10.0,
        *pieces, lag_table,
    )

    weight_half = lax.dynamic_slice_in_dim(weight_out, core * chans, chans, 0)
    below = lax.ppermute(
        weight_half, "section", [(s, (s + 1) % section_count) for s in range(section_count)]
    )
    below, _ = lax.optimization_barrier((below, spectra))
    below_core = swap_core(below)

    spec = pltpu.VMEM((2 * ext, chans), f32)
    total_wide = shape(2 * ext, f32)
    total_scratch = pltpu.VMEM((2 * ext, chans), bf16)
    mixed = pltpu.VMEM((ext + PAD, chans), f32)
    ms = list(range(1, chips // 2))
    specs = pltpu.VMEM((len(ms), 2 * ext, chans), f32)
    late_count = chips - 1 - len(ms)
    late_specs = pltpu.VMEM((2 * ext, late_count * chans), f32)
    side = pltpu.VMEM((rows, late_count * chans), bf16)
    gates = [shape(rows, bf16), shape(own_rows, bf16), shape(own_rows, bf16), shape(PAD, bf16)]
    proj = pltpu.VMEM((ext, 2 * chans), bf16)
    late_outs = [shape(ext, f32, width), shape(ext, bf16, width)]
    ends = [shape(own_rows + PAD, f32, width), shape(own_rows + PAD, bf16, width)]
    result = jnp.zeros((own_rows, width), bf16)
    conv = d_out = ready = None
    for turn in range(section_count):
        first, final = turn == 0, turn == section_count - 1
        upper = section_count - 1 - turn
        if first:
            block, rim, d_out = run(
                gate_grad, [gates[0], gates[-1], shape(ext, f32)], [], "gate_grad", 1.0, grad, grad_core, weight_out, query
            )
        else:
            block, upper_half, lower_half, rim = run(gate_only, gates, [], "gate_only", 0.3, d_out, query, ready)

        def send(value, at, m):
            if first:
                value = jnp.where(((seq_place // 2) ^ m) > seq_place // 2, product[at], value)
            return swap_chip(value, m)

        got = [send(block, slice(0, rows), m) for m in range(1, chips - 1)]
        if first:
            got.append(send(block, slice(0, rows), chips - 1))
        else:
            got.append(send(upper_half, slice(0, own_rows), chips - 1))
            got.append(send(lower_half, slice(own_rows, rows), chips - 1))
        soon, last = got[: len(ms)], got[len(ms) :]
        if not first:
            grad_core = swap_core(grad)
        if first:
            start, start_conv, weight_own = run(
                lambda place, *refs: early_first(place, chips, *refs),
                [total_wide, total_wide, shape(width, bf16, 3 * chans)], [spec], "early_first", 10.0, block, product, spectra, table, weight_in,
            )
            start, start_conv = run(
                lambda place, *refs: middle_first(place, chips, ms, *refs),
                [total_wide, total_wide], [specs], "middle_first", 10.0, *soon, start, start_conv, spectra, table,
            )
            share, short_share, conv = run(
                lambda place, *refs: late_first(place, chips, len(last), *refs),
                late_outs + [shape(ext, bf16)], [late_specs, total_scratch, mixed, proj, side], "late_first", 4.0,
                *last, start, start_conv, d_out, product, block, rim, spectra, table, inverse, keys, values, bias,
                taps, weight_own,
            )
            carried = run(carry_grad, shape(ext, f32), [], "carry_grad", 1.0, grad, grad_core, below, start)
            pass_on = run(pass_half, shape(ext, bf16), [], "pass_half", 0.5, short_share, below_core)
        else:
            start, part_share = run(
                lambda place, *refs: early(place, chips, *refs),
                [total_wide, shape(ext, f32, width)], [spec, mixed, proj], "early", 1.6,
                block, d_out, conv, spectra, table, taps, weight_own,
            )
            start = run(
                lambda place, *refs: middle(place, chips, ms, *refs),
                total_wide, [specs], "middle", 0.8, *soon, start, spectra, table,
            )
            scratch = [late_specs, total_scratch, mixed, proj, side]
            answer = run(
                lambda place, *refs, final=final: late(place, chips, len(last), final, *refs),
                late_outs[:1] if final else late_outs + [shape(ext, bf16)],
                scratch + [pltpu.VMEM((ext, width), bf16)] if final else scratch, "late", 2.5,
                *last, start, part_share, block, rim, spectra, table, inverse, keys, values, bias, taps, weight_own,
                below_core,
            )
            share = answer[0]
            if not final:
                short_share, pass_on = answer[1:]
                carried = run(carry_grad, shape(ext, f32), [], "carry_grad", 0.5, grad, grad_core, below, pass_on)
        half = share if final else pass_on
        if not final:
            keep = run(keep_half, shape(ext, f32), [], "keep_half", 0.6, short_share, below, carried)
            half = (keep + swap_core(pass_on).astype(f32)).astype(bf16)
            d_out = swap_section(half, upper)
        keep_rows, pass_rows = run(split_rows, ends, [], "split_rows", 0.3, share, half)
        ready = (grad.astype(f32) + keep_rows + swap_core(pass_rows).astype(f32)).astype(bf16)
        result = jnp.where(section_place == upper, ready[:own_rows], result)
        if not final:
            grad = swap_section(ready, upper)
    return result[None, None]


def solution(mesh):
    return jax.shard_map(
        shards,
        mesh=mesh,
        in_specs=(
            P(None, "seq", None),
            P("section", None, "seq", None),
            P("section", None, None),
            P("section", None, None),
            P("section", None, None),
            P("section", "seq", None),
            P("section", None),
        ),
        out_specs=P("section", None, "seq", None),
        check_vma=False,
    )
```
